256 devices in a mesh: view: 8 (over x, core), band: 32 (over z, y).
Axes of the slice: x: 4, y: 4, z: 8, core: 2. Of those that a mesh axis runs over, the one named last changes fastest.
Arguments:
- latents: bfloat16 [8, 8192, 1024], P('view', 'band'), may hold values from -170 to 170
- w_qkv: bfloat16 [1024, 3072], replicated, may hold values from -0.75 to 0.75
- w_out: bfloat16 [1024, 1024], replicated, may hold values from -0.1875 to 0.1875
- epipolar_bands: int32 [8, 32, 8], replicated, may hold values from -1 to 31, as said below
- object_token_mask: int32 [8, 8192], replicated, may hold values from 0 to 1, as said below
Outputs:
- updated: float32 [8, 8192, 1024], P('view', 'band')
The draws below stay inside these ranges and needn't reach their ends.
Inputs may be any that keep to these rules, and one draw needn't show every extreme that they name: epipolar_bands[v, b, w] is -1 where w is v or the epipolar lines miss view w; otherwise a band of view w within 2 bands of b. For every query band and every nonzero distance d, at most 2 views have band b + d listed, and some query band lists 2 views at one such distance. `object_token_mask`: the first token of every band is 1.
All inputs are finite; a program needn't handle non-finite values.
Results may differ from the reference program's by a relative error of at most 0.023.
Values may be sent and summed in bfloat16 or wider, within the bound.
A program may use at most 128 MiB of HBM per device.

```python
import jax
import jax.numpy as jnp
from jax import lax

D = 1024
HEADS = 16
HEAD_DIM = 64
TOKENS_PER_BAND = 256
REACH = 2
MOST = 2
VIEW_COUNT = 8
ROW_BAND_COUNT = 32
TOKENS_VIEW = 8192


def draw_latents(key, part):
    key = jax.random.fold_in(key, 5)
    first = jax.random.fold_in(key, 0)
    values = jnp.clip(jax.random.normal(first, (VIEW_COUNT, TOKENS_VIEW, D), jnp.float32), -6.0, 6.0)
    return values.astype(jnp.bfloat16)


def draw_object_token_mask(key, part):
    key = jax.random.fold_in(key, 7)
    first, second = jax.random.split(key)
    level = jax.random.randint(first, (VIEW_COUNT, ROW_BAND_COUNT, 1), 1, 9)
    coin = jax.random.randint(second, (VIEW_COUNT, ROW_BAND_COUNT, TOKENS_PER_BAND), 0, 8)
    first_token = jnp.arange(TOKENS_PER_BAND)[None, None, :] == 0
    live = (coin < level) | first_token
    return jnp.where(live, 1, 0).astype(jnp.int32).reshape(VIEW_COUNT, TOKENS_VIEW)


def draw_epipolar_bands(key, part):
    key = jax.random.fold_in(key, 11)
    first, second = jax.random.split(key)
    view_numbers = jnp.arange(VIEW_COUNT, dtype=jnp.int32)
    band_ids = jnp.arange(ROW_BAND_COUNT, dtype=jnp.int32)[None, :, None]
    offsets = jax.random.randint(first, (VIEW_COUNT, ROW_BAND_COUNT, VIEW_COUNT), -REACH, REACH + 1)
    seen = jax.random.randint(second, (VIEW_COUNT, ROW_BAND_COUNT, VIEW_COUNT), 0, 4) > 0
    destination = jnp.clip(band_ids + offsets, 0, ROW_BAND_COUNT - 1)
    query_view = view_numbers[:, None, None]
    remote_view = view_numbers[None, None, :]
    forced_zone = (query_view == 0) & (band_ids == 0)
    forced = jnp.where((remote_view >= 1) & (remote_view <= MOST), 1, 0)
    destination = jnp.where(forced_zone, forced, destination)
    seen = jnp.where(forced_zone, True, seen)
    seen = seen & (query_view != remote_view)
    same = destination[..., :, None] == destination[..., None, :]
    earlier = view_numbers[None, :] < view_numbers[:, None]
    ranks = jnp.sum((same & seen[..., None, :] & earlier[None, None]).astype(jnp.int32), axis=-1)
    keep = seen & ((destination == band_ids) | (ranks < MOST))
    return jnp.where(keep, destination, -1).astype(jnp.int32)


def bell_draw(own_key, dims, scale, most, held_as=jnp.bfloat16):
    return jnp.clip(scale * jax.random.normal(own_key, dims, jnp.float32), -most, most).astype(held_as)


def setup_inputs(seed: int = 0) -> dict:
    seeds = jax.random.split(jax.random.key(seed), 6)
    latents = draw_latents(jax.random.fold_in(seeds[5], 71), 0)
    w_qkv = bell_draw(seeds[1], (D, 3 * D), (1.7 / D ** 0.5), 0.75)
    w_out = bell_draw(seeds[2], (D, D), D ** -0.5, 0.1875)
    epipolar_bands = draw_epipolar_bands(jax.random.fold_in(seeds[5], 71), 0)
    object_token_mask = draw_object_token_mask(jax.random.fold_in(seeds[5], 71), 0)
    return dict(latents=latents, w_qkv=w_qkv, w_out=w_out, epipolar_bands=epipolar_bands, object_token_mask=object_token_mask)


def attend(queries, key_rows, values, usable):
    count_of_rows = queries.shape[0]
    key_count = key_rows.shape[0]
    query_f = queries.astype(jnp.float32).reshape(count_of_rows, HEADS, HEAD_DIM)
    key_f = key_rows.astype(jnp.float32).reshape(key_count, HEADS, HEAD_DIM)
    value_f = values.astype(jnp.float32).reshape(key_count, HEADS, HEAD_DIM)
    scores = jnp.einsum("qhd,khd->hqk", query_f, key_f) * (HEAD_DIM ** -0.5)
    scores = jnp.where(usable[None, None, :], scores, -1e30)
    row_top = jnp.max(scores, axis=-1, keepdims=True)
    raised = jnp.exp(scores - row_top)
    attention = (raised / jnp.sum(raised, axis=-1, keepdims=True)).astype(jnp.bfloat16)
    blended = jnp.einsum("hqk,khd->qhd", attention.astype(jnp.float32), value_f)
    return blended.reshape(count_of_rows, HEADS * HEAD_DIM).astype(jnp.bfloat16)


def reference(latents, w_qkv, w_out, epipolar_bands, object_token_mask):
    width = latents.shape[2]
    projected = jnp.dot(latents.reshape(VIEW_COUNT * TOKENS_VIEW, width), w_qkv, preferred_element_type=jnp.float32).astype(jnp.bfloat16)
    projected = projected.reshape(VIEW_COUNT, ROW_BAND_COUNT, TOKENS_PER_BAND, 3 * width)
    active_flags = object_token_mask.reshape(VIEW_COUNT, ROW_BAND_COUNT, TOKENS_PER_BAND) > 0

    def one_band(flat_index):
        view_lookup = flat_index // ROW_BAND_COUNT
        band_at = flat_index % ROW_BAND_COUNT
        queries = projected[view_lookup, band_at, :, :width]
        slab_list = []
        active_list = []
        for step_off in (-1, 0, 1):
            destination = band_at + step_off
            clamped_index = jnp.clip(destination, 0, ROW_BAND_COUNT - 1).astype(jnp.int32)
            slab_list.append(projected[view_lookup, clamped_index, :, width:])
            active_list.append(active_flags[view_lookup, clamped_index] & (destination >= 0) & (destination < ROW_BAND_COUNT))
        for remote_view in range(VIEW_COUNT):
            destination = epipolar_bands[view_lookup, band_at, remote_view]
            clamped_index = jnp.clip(destination, 0, ROW_BAND_COUNT - 1).astype(jnp.int32)
            slab_list.append(projected[remote_view, clamped_index, :, width:])
            active_list.append(active_flags[remote_view, clamped_index] & (destination >= 0) & (view_lookup != remote_view))
        slabs = jnp.concatenate(slab_list, axis=0)
        usable = jnp.concatenate(active_list, axis=0)
        return attend(queries, slabs[:, :width], slabs[:, width:], usable)

    blended = lax.map(one_band, jnp.arange(VIEW_COUNT * ROW_BAND_COUNT, dtype=jnp.int32))
    blended = blended.reshape(VIEW_COUNT * TOKENS_VIEW, width)
    updated = latents.reshape(VIEW_COUNT * TOKENS_VIEW, width).astype(jnp.float32) + jnp.dot(blended, w_out, preferred_element_type=jnp.float32)
    return updated.reshape(VIEW_COUNT, TOKENS_VIEW, width)
```

```python
import functools

import jax
import jax.numpy as jnp
from jax import lax
from jax.experimental import pallas as pl
from jax.experimental.pallas import tpu as pltpu
from jax.sharding import PartitionSpec as P

MESH = pl.DeviceIdType.MESH
HEAD_DIM = 64
REACH = 2
NEAR = 3
FAR = 4
BIG = -1e30
VALID = 64


def exchange_plan(chips):
    order = [0] + sorted(range(1, chips), key=lambda o: -min(o, chips - o))
    return order


def kernel(
    views, bands, table, lat, w_qkv, w_out, mask, out,
    w_buf, wo_buf, mask_buf, kv_send, q_send, kv_near, kv_far, q_buf, k_cat, v_cat,
    acc_buf, top_buf, o_send, o_buf,
    w_sem, wo_sem, mask_sem, kv_ssem, kv_rsem, up_ssem, up_rsem, down_ssem, down_rsem,
    up2_ssem, up2_rsem, down2_ssem, down2_rsem, q_ssem, q_rsem, o_ssem, o_rsem,
):
    tokens, width = lat.shape
    cols = width // views
    pair = 2 * cols
    chips = views // 2
    me = lax.axis_index("view")
    band = lax.axis_index("band")
    chip, core = me // 2, me % 2
    above, below = (band + 1) % bands, (band + bands - 1) % bands

    barrier = pltpu.get_barrier_semaphore()
    for off in range(1, views):
        pl.semaphore_signal(barrier, 1, device_id=((me + off) % views, band), device_id_type=MESH)
    for other in (above, below):
        pl.semaphore_signal(barrier, 1, device_id=(me, other), device_id_type=MESH)

    order = exchange_plan(chips)
    loads = []
    for n, off in enumerate(order):
        there = (chip + off) % chips
        for part in (1, 2, 0):
            load = pltpu.make_async_copy(
                w_qkv.at[:, pl.ds(pl.multiple_of(part * width + there * pair, pair), pair)],
                w_buf.at[n, part],
                w_sem.at[n, part],
            )
            load.start()
            loads.append(load)
    masks = []
    for n, d in enumerate((-1, 0, 1, -2, 2)):
        at = jnp.clip(band + d, 0, bands - 1)
        load = pltpu.make_async_copy(
            mask.at[:, pl.ds(pl.multiple_of(at * tokens, tokens), tokens)],
            mask_buf.at[pl.ds(n * views, views)],
            mask_sem.at[n],
        )
        load.start()
        masks.append(load)
    wo_load = pltpu.make_async_copy(w_out, wo_buf, wo_sem)
    wo_load.start()

    def copy(src, dst, ssem, rsem, view, at):
        return pltpu.make_async_remote_copy(
            src_ref=src, dst_ref=dst, send_sem=ssem, recv_sem=rsem,
            device_id=(view, at), device_id_type=MESH,
        )

    def kv_to(view):
        return copy(kv_send.at[view], kv_near.at[views + me], kv_ssem.at[view], kv_rsem.at[me], view, band)

    def q_to(view):
        return copy(q_send.at[view], q_buf.at[me], q_ssem.at[view], q_rsem.at[me], view, band)

    def kv_from(view):
        return copy(kv_send.at[view], kv_near.at[views + view], kv_ssem.at[view], kv_rsem.at[view], view, band)

    def q_from(view):
        return copy(q_send.at[view], q_buf.at[view], q_ssem.at[view], q_rsem.at[view], view, band)

    def up(view):
        return copy(kv_near.at[views + view], kv_near.at[view], up_ssem.at[view], up_rsem.at[view], me, above)

    def down(view):
        return copy(kv_near.at[views + view], kv_near.at[2 * views + view], down_ssem.at[view], down_rsem.at[view], me, below)

    def up2(view):
        return copy(kv_near.at[view], kv_far.at[view], up2_ssem.at[view], up2_rsem.at[view], me, above)

    def down2(view):
        return copy(kv_near.at[2 * views + view], kv_far.at[views + view], down2_ssem.at[view], down2_rsem.at[view], me, below)

    row = lat[...]
    scale = HEAD_DIM**-0.5

    def project(n, part):
        loads[3 * n + {1: 0, 2: 1, 0: 2}[part]].wait()
        return jnp.dot(row, w_buf[n, part], preferred_element_type=jnp.float32).astype(jnp.bfloat16)

    def put_pair(there, part, value):
        for c in range(2):
            kv_send[2 * there + c, part] = value[:, c * cols : (c + 1) * cols]

    for n, off in enumerate(order):
        there = (chip + off) % chips
        put_pair(there, 0, project(n, 1))
        put_pair(there, 1, project(n, 2))
        if n == 0:
            kv_near[views + me] = kv_send[me]
            pl.semaphore_wait(barrier, views + 1)
            up(me).start()
            down(me).start()
            kv_to(2 * chip + 1 - core).start()
        else:
            for c in range(2):
                kv_to(2 * there + c).start()
        queries = project(n, 0) * jnp.bfloat16(scale)
        for c in range(2):
            q_send[2 * there + c] = queries[:, c * cols : (c + 1) * cols]
        if n == 0:
            q_buf[me] = q_send[me]

    others = [2 * chip + 1 - core]
    for off in sorted(range(1, chips), key=lambda o: min(o, chips - o)):
        others += [2 * ((chip + off) % chips) + c for c in range(2)]
    for view in reversed(others):
        q_to(view).start()
    for view in others:
        kv_from(view).wait_recv()
        up(view).start()
        down(view).start()
    for view in [me, *others]:
        up(view).wait_recv()
        up2(view).start()
        down(view).wait_recv()
        down2(view).start()
    for load in masks:
        load.wait()
    for view in others:
        q_from(view).wait_recv()

    v_cat[:, cols:] = jnp.ones((v_cat.shape[0], cols), jnp.bfloat16)
    lane = lax.broadcasted_iota(jnp.int32, (tokens, cols), 1)

    def bias_row(index, valid):
        seen = mask_buf[pl.ds(index, 1), :] * valid
        return jnp.where(seen > 0, 0.0, BIG)

    def attend(view, bias, keys):
        q = q_buf[view]
        results = []
        for h in range(2):
            mine = lane // HEAD_DIM == h
            qh = jnp.where(mine, q, jnp.zeros_like(q))
            s = lax.dot_general(
                qh, k_cat[:keys], (((1,), (1,)), ((), ())), preferred_element_type=jnp.float32
            )
            s = s + bias
            top = jnp.max(s, axis=1, keepdims=True)
            p = jnp.exp(s - top).astype(jnp.bfloat16)
            results.append((jnp.dot(p, v_cat[:keys], preferred_element_type=jnp.float32), top))
        return results

    def near_step(i, carry):
        view = (me + 1 + i) % views
        rows = []
        up_ok = jnp.where(band > 0, 1, 0)
        down_ok = jnp.where(band < bands - 1, 1, 0)
        spots = [(views + view, 1), (view, up_ok), (2 * views + view, down_ok)]
        for r in range(NEAR):
            code = table[view, r]
            spots.append((code % VALID, code // VALID))
        for n, (index, valid) in enumerate(spots):
            k_cat[n * tokens : (n + 1) * tokens] = kv_near[index, 0]
            v_cat[n * tokens : (n + 1) * tokens, :cols] = kv_near[index, 1]
            rows.append(bias_row(index, valid))
        for h, (acc, top) in enumerate(attend(view, jnp.concatenate(rows, axis=1), (3 + NEAR) * tokens)):
            acc_buf[i, h] = acc
            top_buf[i, h] = jnp.broadcast_to(top, (tokens, cols))
        return carry

    lax.fori_loop(0, views, near_step, 0)

    for view in [me, *others]:
        up2(view).wait_recv()
        down2(view).wait_recv()

    def far_step(i, carry):
        view = (me + 1 + i) % views
        rows = []
        for n in range(FAR):
            code = table[view, NEAR + n]
            index, valid = code % VALID, code // VALID
            near_index = jnp.minimum(index, 3 * views - 1)
            far_index = jnp.maximum(index - 3 * views, 0)
            is_near = index < 3 * views
            k_cat[n * tokens : (n + 1) * tokens] = jnp.where(is_near, kv_near[near_index, 0], kv_far[far_index, 0])
            v_cat[n * tokens : (n + 1) * tokens, :cols] = jnp.where(
                is_near, kv_near[near_index, 1], kv_far[far_index, 1]
            )
            rows.append(bias_row(index, valid))
        blends = []
        for h, (acc, top) in enumerate(attend(view, jnp.concatenate(rows, axis=1), FAR * tokens)):
            old = top_buf[i, h][:, :1]
            new = jnp.maximum(old, top)
            total = acc_buf[i, h] * jnp.exp(old - new) + acc * jnp.exp(top - new)
            blends.append(total[:, :cols] / total[:, cols:])
        blend = jnp.where(lane < HEAD_DIM, blends[0], blends[1]).astype(jnp.bfloat16)
        o_send[view] = blend

        @pl.when(i < views - 1)
        def _():
            copy(o_send.at[view], o_buf.at[me], o_ssem.at[view], o_rsem.at[me], view, band).start()

        return carry

    lax.fori_loop(0, views, far_step, 0)
    o_buf[me] = o_send[me]
    wo_load.wait()
    for view in others:
        copy(o_send.at[view], o_buf.at[view], o_ssem.at[view], o_rsem.at[view], view, band).wait_recv()
    total = row.astype(jnp.float32)
    for c in range(chips):
        both = jnp.concatenate([o_buf[2 * c], o_buf[2 * c + 1]], axis=1)
        total = total + jnp.dot(both, wo_buf[c * pair : (c + 1) * pair], preferred_element_type=jnp.float32)
    out[...] = total

    for view in others:
        kv_to(view).wait_send()
        q_to(view).wait_send()
        copy(o_send.at[view], o_buf.at[me], o_ssem.at[view], o_rsem.at[me], view, band).wait_send()
    for view in [me, *others]:
        for way in (up, down, up2, down2):
            way(view).wait_send()


def epipolar_table(epipolar_bands, band, views):
    listed = lax.dynamic_index_in_dim(epipolar_bands, band, axis=1, keepdims=False)
    far = listed - band
    numbers = jnp.arange(views, dtype=jnp.int32)
    own = numbers[:, None] == numbers[None, :]
    present = (listed >= 0) & ~own
    slot = jnp.where(far == -2, 3, jnp.where(far == 2, 4, jnp.clip(far, -1, 1) + 1))
    code = jnp.where(present, slot * views + numbers[None, :] + VALID, views + numbers[None, :])
    key = jnp.where(own, REACH + 1, jnp.where(present, jnp.abs(far), 0)) * views + numbers[None, :]
    rank = jnp.sum((key[:, None, :] < key[:, :, None]).astype(jnp.int32), axis=2)
    return jnp.sum(jnp.where(rank[:, :, None] == numbers[None, None, :], code[:, :, None], 0), axis=1)


def body(latents, w_qkv, w_out, epipolar_bands, object_token_mask):
    views = lax.axis_size("view")
    bands = lax.axis_size("band")
    tokens, width = latents.shape[1:]
    cols = width // views
    table = epipolar_table(epipolar_bands, lax.axis_index("band"), views)
    bf16, f32 = jnp.bfloat16, jnp.float32
    dma = pltpu.SemaphoreType.DMA
    vmem = pl.BlockSpec(memory_space=pltpu.VMEM)
    hbm = pl.BlockSpec(memory_space=pltpu.HBM)
    updated = pl.pallas_call(
        functools.partial(kernel, views, bands),
        out_shape=jax.ShapeDtypeStruct((tokens, width), f32),
        in_specs=[pl.BlockSpec(memory_space=pltpu.SMEM), vmem, hbm, hbm, hbm],
        out_specs=vmem,
        scratch_shapes=[
            pltpu.VMEM((views // 2, 3, width, 2 * cols), bf16),
            pltpu.VMEM((width, width), bf16),
            pltpu.VMEM((5 * views, tokens), jnp.int32),
            pltpu.VMEM((views, 2, tokens, cols), bf16),
            pltpu.VMEM((views, tokens, cols), bf16),
            pltpu.VMEM((3 * views, 2, tokens, cols), bf16),
            pltpu.VMEM((2 * views, 2, tokens, cols), bf16),
            pltpu.VMEM((views, tokens, cols), bf16),
            pltpu.VMEM(((3 + NEAR) * tokens, cols), bf16),
            pltpu.VMEM(((3 + NEAR) * tokens, 2 * cols), bf16),
            pltpu.VMEM((views, 2, tokens, 2 * cols), f32),
            pltpu.VMEM((views, 2, tokens, cols), f32),
            pltpu.VMEM((views, tokens, cols), bf16),
            pltpu.VMEM((views, tokens, cols), bf16),
            dma((views // 2, 3)),
            dma,
            dma((5,)),
            *[dma((views,)) for _ in range(14)],
        ],
        compiler_params=pltpu.CompilerParams(
            collective_id=0, has_side_effects=True, vmem_limit_bytes=60 * 2**20
        ),
    )(table, latents[0], w_qkv, w_out, object_token_mask)
    return updated[None]


def solution(mesh):
    placed = (P("view", "band", None), P(), P(), P(), P())
    return jax.shard_map(
        body, mesh=mesh, in_specs=placed, out_specs=P("view", "band", None), check_vma=False
    )
```

```python
import functools

import jax
import jax.numpy as jnp
from jax import lax
from jax.experimental import pallas as pl
from jax.experimental.pallas import tpu as pltpu
from jax.sharding import PartitionSpec as P

MESH = pl.DeviceIdType.MESH
HEAD_DIM = 64
REACH = 2
NEAR = 3
FAR = 4
RING = 4
BIG = -1e30
VALID = 64


def exchange_plan(chips):
    order = [0] + sorted(range(1, chips), key=lambda o: -min(o, chips - o))
    return order


def kernel(
    views, bands, table, lat, w_qkv, w_out, mask, out,
    w_buf, wo_buf, mask_buf, kv_send, q_send, kv_near, kv_far, q_buf, k_cat, v_cat,
    acc_buf, top_buf, o_send, o_buf,
    w_sem, wo_sem, mask_sem, kv_ssem, kv_rsem, up_ssem, up_rsem, down_ssem, down_rsem,
    hop_ssem, cross_ssem, far_rsem, q_ssem, q_rsem, o_ssem, o_rsem,
):
    tokens, width = lat.shape
    cols = width // views
    pair = 2 * cols
    chips = views // 2
    me = lax.axis_index("view")
    band = lax.axis_index("band")
    chip, core = me // 2, me % 2
    above, below = (band + 1) % bands, (band + bands - 1) % bands
    place = band % RING
    edge, upper, odd = ((place + 1) // 2 + 1) % 2, place // 2, place % 2
    first, last = edge * (1 - upper), edge * upper
    over, under = (band + RING) % bands, (band + bands - RING) % bands
    across = (band + bands + (3 - 2 * place)) % bands

    barrier = pltpu.get_barrier_semaphore()
    for off in range(1, views):
        pl.semaphore_signal(barrier, 1, device_id=((me + off) % views, band), device_id_type=MESH)
    for other in (above, below, over, under, across):
        pl.semaphore_signal(barrier, 1, device_id=(me, other), device_id_type=MESH)

    order = exchange_plan(chips)
    loads = []
    for n, off in enumerate(order):
        there = (chip + off) % chips
        for part in (1, 2, 0):
            load = pltpu.make_async_copy(
                w_qkv.at[:, pl.ds(pl.multiple_of(part * width + there * pair, pair), pair)],
                w_buf.at[n, part],
                w_sem.at[n, part],
            )
            load.start()
            loads.append(load)
    masks = []
    for n, d in enumerate((-1, 0, 1, -2, 2)):
        at = jnp.clip(band + d, 0, bands - 1)
        load = pltpu.make_async_copy(
            mask.at[:, pl.ds(pl.multiple_of(at * tokens, tokens), tokens)],
            mask_buf.at[pl.ds(n * views, views)],
            mask_sem.at[n],
        )
        load.start()
        masks.append(load)
    wo_load = pltpu.make_async_copy(w_out, wo_buf, wo_sem)
    wo_load.start()

    def copy(src, dst, ssem, rsem, view, at):
        return pltpu.make_async_remote_copy(
            src_ref=src, dst_ref=dst, send_sem=ssem, recv_sem=rsem,
            device_id=(view, at), device_id_type=MESH,
        )

    def kv_to(view):
        return copy(kv_send.at[view], kv_near.at[views + me], kv_ssem.at[view], kv_rsem.at[me], view, band)

    def q_to(view):
        return copy(q_send.at[view], q_buf.at[me], q_ssem.at[view], q_rsem.at[me], view, band)

    def kv_from(view):
        return copy(kv_send.at[view], kv_near.at[views + view], kv_ssem.at[view], kv_rsem.at[view], view, band)

    def q_from(view):
        return copy(q_send.at[view], q_buf.at[view], q_ssem.at[view], q_rsem.at[view], view, band)

    def up(view):
        return copy(kv_near.at[views + view], kv_near.at[view], up_ssem.at[view], up_rsem.at[view], me, above)

    def down(view):
        return copy(kv_near.at[views + view], kv_near.at[2 * views + view], down_ssem.at[view], down_rsem.at[view], me, below)

    def hop_down(view):
        return copy(
            kv_near.at[2 * views + view, edge], kv_far.at[(1 - first) * views + view, edge], hop_ssem.at[0, view],
            far_rsem.at[1 - first, edge, view], me, (band + bands - 1 + RING * first) % bands,
        )

    def hop_up(view):
        return copy(
            kv_near.at[view, edge], kv_far.at[last * views + view, edge], hop_ssem.at[1, view],
            far_rsem.at[last, edge, view], me, (band + bands + 1 - RING * last) % bands,
        )

    def cross(view, half):
        back = upper if half == 0 else odd
        return copy(
            kv_far.at[(1 - back) * views + view, half], kv_far.at[back * views + view, half], cross_ssem.at[half, view],
            far_rsem.at[back, half, view], me, (band + bands + RING * (1 - 2 * back)) % bands,
        )

    def hop_arrival(view, half):
        back = upper if half == 0 else odd
        at = kv_far.at[(1 - back) * views + view, half]
        return copy(at, at, cross_ssem.at[half, view], far_rsem.at[1 - back, half, view], me, above)

    row = lat[...]
    scale = HEAD_DIM**-0.5

    def project(n, part):
        loads[3 * n + {1: 0, 2: 1, 0: 2}[part]].wait()
        return jnp.dot(row, w_buf[n, part], preferred_element_type=jnp.float32).astype(jnp.bfloat16)

    def put_pair(there, part, value):
        for c in range(2):
            for half in range(2):
                kv_send[2 * there + c, half, part] = value[
                    half * tokens // 2 : (half + 1) * tokens // 2, c * cols : (c + 1) * cols
                ]

    for n, off in enumerate(order):
        there = (chip + off) % chips
        put_pair(there, 0, project(n, 1))
        put_pair(there, 1, project(n, 2))
        if n == 0:
            kv_near[views + me] = kv_send[me]
            pl.semaphore_wait(barrier, views + 4)
            up(me).start()
            down(me).start()
            kv_to(2 * chip + 1 - core).start()
        else:
            for c in range(2):
                kv_to(2 * there + c).start()
        queries = project(n, 0) * jnp.bfloat16(scale)
        for c in range(2):
            q_send[2 * there + c] = queries[:, c * cols : (c + 1) * cols]
        if n == 0:
            q_buf[me] = q_send[me]

    others = [2 * chip + 1 - core]
    for off in sorted(range(1, chips), key=lambda o: min(o, chips - o)):
        others += [2 * ((chip + off) % chips) + c for c in range(2)]
    for view in reversed(others):
        q_to(view).start()

    def to_neighbours(view):
        kv_from(view).wait_recv()
        up(view).start()
        down(view).start()

    def hop_on(view):
        up(view).wait_recv()
        hop_up(view).start()
        down(view).wait_recv()
        hop_down(view).start()

    to_neighbours(others[0])
    for view in (me, others[0]):
        hop_on(view)
    for view in others[1:]:
        to_neighbours(view)
    for view in others[1:]:
        hop_on(view)
    for load in masks:
        load.wait()
    for view in others:
        q_from(view).wait_recv()

    v_cat[:, cols:] = jnp.ones((v_cat.shape[0], cols), jnp.bfloat16)
    lane = lax.broadcasted_iota(jnp.int32, (tokens, cols), 1)

    def bias_row(index, valid):
        seen = mask_buf[pl.ds(index, 1), :] * valid
        return jnp.where(seen > 0, 0.0, BIG)

    def attend(view, bias, keys):
        q = q_buf[view]
        results = []
        for h in range(2):
            mine = lane // HEAD_DIM == h
            qh = jnp.where(mine, q, jnp.zeros_like(q))
            s = lax.dot_general(
                qh, k_cat[:keys], (((1,), (1,)), ((), ())), preferred_element_type=jnp.float32
            )
            s = s + bias
            top = jnp.max(s, axis=1, keepdims=True)
            p = jnp.exp(s - top).astype(jnp.bfloat16)
            results.append((jnp.dot(p, v_cat[:keys], preferred_element_type=jnp.float32), top))
        return results

    def near_step(i, carry):
        view = (me + 1 + i) % views
        rows = []
        up_ok = jnp.where(band > 0, 1, 0)
        down_ok = jnp.where(band < bands - 1, 1, 0)
        spots = [(views + view, 1), (view, up_ok), (2 * views + view, down_ok)]
        for r in range(NEAR):
            code = table[view, r]
            spots.append((code % VALID, code // VALID))
        for n, (index, valid) in enumerate(spots):
            for half in range(2):
                at = pl.ds(n * tokens + half * tokens // 2, tokens // 2)
                k_cat[at] = kv_near[index, half, 0]
                v_cat[at, :cols] = kv_near[index, half, 1]
            rows.append(bias_row(index, valid))
        for h, (acc, top) in enumerate(attend(view, jnp.concatenate(rows, axis=1), (3 + NEAR) * tokens)):
            acc_buf[i, h] = acc
            top_buf[i, h] = jnp.broadcast_to(top, (tokens, cols))
        step = i // 2
        sent = 2 * ((chip + step + step // 2 - 2 * (step // 3)) % chips) + (core + i) % 2
        for half in range(2):
            hop_arrival(sent, half).wait_recv()
            cross(sent, half).start()
        return carry

    lax.fori_loop(0, views, near_step, 0)

    for view in [me, *others]:
        for half in range(2):
            cross(view, half).wait_recv()

    def far_step(i, carry):
        view = (me + 1 + i) % views
        rows = []
        for n in range(FAR):
            code = table[view, NEAR + n]
            index, valid = code % VALID, code // VALID
            near_index = jnp.minimum(index, 3 * views - 1)
            far_index = jnp.maximum(index - 3 * views, 0)
            is_near = index < 3 * views
            for half in range(2):
                at = pl.ds(n * tokens + half * tokens // 2, tokens // 2)
                k_cat[at] = jnp.where(is_near, kv_near[near_index, half, 0], kv_far[far_index, half, 0])
                v_cat[at, :cols] = jnp.where(is_near, kv_near[near_index, half, 1], kv_far[far_index, half, 1])
            rows.append(bias_row(index, valid))
        blends = []
        for h, (acc, top) in enumerate(attend(view, jnp.concatenate(rows, axis=1), FAR * tokens)):
            old = top_buf[i, h][:, :1]
            new = jnp.maximum(old, top)
            total = acc_buf[i, h] * jnp.exp(old - new) + acc * jnp.exp(top - new)
            blends.append(total[:, :cols] / total[:, cols:])
        blend = jnp.where(lane < HEAD_DIM, blends[0], blends[1]).astype(jnp.bfloat16)
        o_send[view] = blend

        @pl.when(i < views - 1)
        def _():
            copy(o_send.at[view], o_buf.at[me], o_ssem.at[view], o_rsem.at[me], view, band).start()

        return carry

    lax.fori_loop(0, views, far_step, 0)
    o_buf[me] = o_send[me]
    wo_load.wait()
    for view in others:
        copy(o_send.at[view], o_buf.at[view], o_ssem.at[view], o_rsem.at[view], view, band).wait_recv()
    total = row.astype(jnp.float32)
    for c in range(chips):
        both = jnp.concatenate([o_buf[2 * c], o_buf[2 * c + 1]], axis=1)
        total = total + jnp.dot(both, wo_buf[c * pair : (c + 1) * pair], preferred_element_type=jnp.float32)
    out[...] = total

    for view in others:
        kv_to(view).wait_send()
        q_to(view).wait_send()
        copy(o_send.at[view], o_buf.at[me], o_ssem.at[view], o_rsem.at[me], view, band).wait_send()
    for view in [me, *others]:
        for way in (up, down, hop_up, hop_down):
            way(view).wait_send()
        for half in range(2):
            cross(view, half).wait_send()


def epipolar_table(epipolar_bands, band, views):
    listed = lax.dynamic_index_in_dim(epipolar_bands, band, axis=1, keepdims=False)
    far = listed - band
    numbers = jnp.arange(views, dtype=jnp.int32)
    own = numbers[:, None] == numbers[None, :]
    present = (listed >= 0) & ~own
    slot = jnp.where(far == -2, 3, jnp.where(far == 2, 4, jnp.clip(far, -1, 1) + 1))
    code = jnp.where(present, slot * views + numbers[None, :] + VALID, views + numbers[None, :])
    key = jnp.where(own, REACH + 1, jnp.where(present, jnp.abs(far), 0)) * views + numbers[None, :]
    rank = jnp.sum((key[:, None, :] < key[:, :, None]).astype(jnp.int32), axis=2)
    return jnp.sum(jnp.where(rank[:, :, None] == numbers[None, None, :], code[:, :, None], 0), axis=1)


def body(latents, w_qkv, w_out, epipolar_bands, object_token_mask):
    views = lax.axis_size("view")
    bands = lax.axis_size("band")
    tokens, width = latents.shape[1:]
    cols = width // views
    table = epipolar_table(epipolar_bands, lax.axis_index("band"), views)
    bf16, f32 = jnp.bfloat16, jnp.float32
    dma = pltpu.SemaphoreType.DMA
    vmem = pl.BlockSpec(memory_space=pltpu.VMEM)
    hbm = pl.BlockSpec(memory_space=pltpu.HBM)
    updated = pl.pallas_call(
        functools.partial(kernel, views, bands),
        out_shape=jax.ShapeDtypeStruct((tokens, width), f32),
        in_specs=[pl.BlockSpec(memory_space=pltpu.SMEM), vmem, hbm, hbm, hbm],
        out_specs=vmem,
        scratch_shapes=[
            pltpu.VMEM((views // 2, 3, width, 2 * cols), bf16),
            pltpu.VMEM((width, width), bf16),
            pltpu.VMEM((5 * views, tokens), jnp.int32),
            pltpu.VMEM((views, 2, 2, tokens // 2, cols), bf16),
            pltpu.VMEM((views, tokens, cols), bf16),
            pltpu.VMEM((3 * views, 2, 2, tokens // 2, cols), bf16),
            pltpu.VMEM((2 * views, 2, 2, tokens // 2, cols), bf16),
            pltpu.VMEM((views, tokens, cols), bf16),
            pltpu.VMEM(((3 + NEAR) * tokens, cols), bf16),
            pltpu.VMEM(((3 + NEAR) * tokens, 2 * cols), bf16),
            pltpu.VMEM((views, 2, tokens, 2 * cols), f32),
            pltpu.VMEM((views, 2, tokens, cols), f32),
            pltpu.VMEM((views, tokens, cols), bf16),
            pltpu.VMEM((views, tokens, cols), bf16),
            dma((views // 2, 3)),
            dma,
            dma((5,)),
            *[dma((views,)) for _ in range(6)],
            dma((2, views)),
            dma((2, views)),
            dma((2, 2, views)),
            *[dma((views,)) for _ in range(4)],
        ],
        compiler_params=pltpu.CompilerParams(
            collective_id=0, has_side_effects=True, vmem_limit_bytes=60 * 2**20
        ),
    )(table, latents[0], w_qkv, w_out, object_token_mask)
    return updated[None]


def solution(mesh):
    placed = (P("view", "band", None), P(), P(), P(), P())
    return jax.shard_map(
        body, mesh=mesh, in_specs=placed, out_specs=P("view", "band", None), check_vma=False
    )
```

```python
import functools
import itertools

import jax
import jax.numpy as jnp
from jax import lax
from jax.experimental import pallas as pl
from jax.experimental.pallas import tpu as pltpu
from jax.sharding import PartitionSpec as P

MESH = pl.DeviceIdType.MESH
HEAD_DIM = 64
RING = 4
LISTED = 7
HARD = 3
EASY = 5
LAG = 4
BIG = -1e30
VALID = 64


def kernel(
    views, bands, table, lat, w_qkv, w_out, mask, out,
    w_buf, wo_buf, mask_buf, kv_send, q_send, kv_near, kv_far, q_buf, cat,
    acc_buf, top_buf, o_send, o_buf,
    w_sem, wo_sem, mask_sem, kv_ssem, kv_rsem, q_ssem, q_rsem, halo_ssem, halo_rsem, cross_ssem, cross_rsem,
    o_ssem, o_rsem,
):
    tokens, width = lat.shape
    part_rows = tokens // 2
    cols = width // views
    wide = 2 * cols
    chips = views // 2
    me = lax.axis_index("view")
    band = lax.axis_index("band")
    chip, core = me // 2, me % 2
    place = band % RING
    upper, odd = place // 2, place % 2
    head = (odd + upper) % 2
    base = band - odd
    partner = band + 1 - 2 * odd
    across = band + 3 - 2 * place
    over, under = (band + RING) % bands, (band + bands - RING) % bands
    beyond = (band + bands + RING * (1 - 2 * upper)) % bands

    def visit(step):
        near = step // 2 % chips
        return 2 * ((chip + near + near // 2 - 2 * (near // 3)) % chips) + (core + step) % 2

    loads = {}

    def fetch(part, n):
        there = visit(2 * n) // 2
        load = pltpu.make_async_copy(
            w_qkv.at[:, pl.ds(pl.multiple_of(part * width + there * wide, wide), wide)],
            w_buf.at[n, part],
            w_sem.at[n, part],
        )
        load.start()
        loads[n, part] = load

    for n, part in itertools.product(range(chips), (1, 2)):
        fetch(part, n)

    barrier = pltpu.get_barrier_semaphore()
    for off in range(1, views):
        for row in (band, partner):
            pl.semaphore_signal(barrier, 1, device_id=((me + off) % views, row), device_id_type=MESH)
    for row in (partner, across, over, under):
        pl.semaphore_signal(barrier, 1, device_id=(me, row), device_id_type=MESH)

    for n in range(chips):
        fetch(0, n)
    masks = []
    side = 2 - 4 * upper
    for group, shift in enumerate((0, side, -side)):
        for j in range(2):
            at = jnp.clip(base + shift + j, 0, bands - 1)
            load = pltpu.make_async_copy(
                mask.at[:, pl.ds(pl.multiple_of(at * tokens, tokens), tokens)],
                mask_buf.at[pl.ds((2 * group + j) * views, views)],
                mask_sem.at[2 * group + j],
            )
            load.start()
            masks.append(load)
    wo_load = pltpu.make_async_copy(w_out, wo_buf, wo_sem)
    wo_load.start()

    def copy(src, dst, ssem, rsem, view, at):
        return pltpu.make_async_remote_copy(
            src_ref=src, dst_ref=dst, send_sem=ssem, recv_sem=rsem,
            device_id=(view, at), device_id_type=MESH,
        )

    def kv_to(view, theirs):
        h = (head + theirs) % 2
        return copy(
            kv_send.at[view, h], kv_near.at[odd, me], kv_ssem.at[view, h], kv_rsem.at[odd, me],
            view, partner if theirs else band,
        )

    def q_to(view, theirs):
        h = (head + theirs) % 2
        return copy(
            q_send.at[view, h], q_buf.at[odd, me], q_ssem.at[view, h], q_rsem.at[odd, me],
            view, partner if theirs else band,
        )

    def kv_from(view, theirs):
        j = (odd + theirs) % 2
        at = kv_near.at[j, view]
        return copy(at, at, kv_ssem.at[view, 0], kv_rsem.at[j, view], me, partner)

    def q_from(view, theirs):
        j = (odd + theirs) % 2
        at = q_buf.at[j, view]
        return copy(at, at, q_ssem.at[view, 0], q_rsem.at[j, view], me, partner)

    def halo(view):
        return copy(
            kv_near.at[pl.ds(0, 2), view], kv_near.at[pl.ds(2, 2), view], halo_ssem.at[view], halo_rsem.at[view],
            me, across,
        )

    def cross(view):
        return copy(
            kv_near.at[pl.ds(2, 2), view], kv_far.at[pl.ds(0, 2), view], cross_ssem.at[view], cross_rsem.at[view],
            me, beyond,
        )

    def o_to(view, j):
        return copy(
            o_send.at[j, view], o_buf.at[2 * me + head], o_ssem.at[j, view], o_rsem.at[2 * me + head], view, base + j
        )

    def o_from(view, theirs):
        slot = 2 * view + (head + theirs) % 2
        at = o_buf.at[slot]
        return copy(at, at, o_ssem.at[0, view], o_rsem.at[slot], me, partner)

    row = lat[...]
    scale = HEAD_DIM**-0.5
    low = lax.broadcasted_iota(jnp.int32, (tokens, cols), 1) < HEAD_DIM
    low_part = lax.broadcasted_iota(jnp.int32, (part_rows, cols), 1) < HEAD_DIM

    def turn(x):
        return pltpu.roll(x, HEAD_DIM, 1)

    def project(n, part):
        loads[n, part].wait()
        return jnp.dot(row, w_buf[n, part], preferred_element_type=jnp.float32)

    others = [visit(step) for step in range(1, views)]

    for n in range(chips):
        there = visit(2 * n) // 2
        keys, values = project(n, 1), project(n, 2)
        for c in range(2):
            k = keys[:, c * cols : (c + 1) * cols]
            v = values[:, c * cols : (c + 1) * cols]
            kv_send[2 * there + c, 0] = jnp.where(low, k, turn(v)).astype(jnp.bfloat16)
            kv_send[2 * there + c, 1] = jnp.where(low, turn(k), v).astype(jnp.bfloat16)
        if n == 0:
            kv_near[odd, me] = kv_send[me, head]
            pl.semaphore_wait(barrier, 2 * views + 2)
            kv_to(me, 1).start()
            for theirs in range(2):
                kv_to(2 * chip + 1 - core, theirs).start()
        else:
            for c, theirs in itertools.product(range(2), range(2)):
                kv_to(2 * there + c, theirs).start()
    for n in range(chips):
        there = visit(2 * n) // 2
        queries = project(n, 0) * scale
        for c in range(2):
            first = queries[:part_rows, c * cols : (c + 1) * cols]
            second = queries[part_rows:, c * cols : (c + 1) * cols]
            q_send[2 * there + c, 0] = jnp.where(low_part, first, turn(second)).astype(jnp.bfloat16)
            q_send[2 * there + c, 1] = jnp.where(low_part, turn(first), second).astype(jnp.bfloat16)
        if n == 0:
            q_buf[odd, me] = q_send[me, head]
            q_to(me, 1).start()
            for theirs in range(2):
                q_to(2 * chip + 1 - core, theirs).start()
        else:
            for c, theirs in itertools.product(range(2), range(2)):
                q_to(2 * there + c, theirs).start()

    for load in masks:
        load.wait()
    cat[:, cols:] = jnp.ones((cat.shape[0], cols), jnp.bfloat16)

    def bias_row(index, valid):
        seen = mask_buf[pl.ds(index, 1), :] * valid
        return jnp.where(seen > 0, 0.0, BIG)

    def query(j, view):
        both = q_buf[j, view].astype(jnp.float32)
        rows = jnp.concatenate([jnp.where(low_part, both, 0.0), jnp.where(low_part, turn(both), 0.0)], axis=0)
        return rows.astype(jnp.bfloat16)

    def attend(q, rows, count):
        keys = count * tokens
        s = lax.dot_general(
            q, cat[:keys, :cols], (((1,), (1,)), ((), ())), preferred_element_type=jnp.float32
        )
        s = s + jnp.concatenate(rows, axis=1)
        top = jnp.max(s, axis=1, keepdims=True)
        p = jnp.exp(s - top).astype(jnp.bfloat16)
        return jnp.dot(p, cat[:keys], preferred_element_type=jnp.float32), top

    def store(j, view, acc, top):
        acc_buf[j, view] = acc
        top_buf[j, view] = jnp.broadcast_to(top, (tokens, cols))

    def merge(j, view, acc, top):
        old = top_buf[j, view][:, :1]
        new = jnp.maximum(old, top)
        return acc_buf[j, view] * jnp.exp(old - new) + acc * jnp.exp(top - new), new

    def put(n, slab):
        cat[n * tokens : (n + 1) * tokens, :cols] = slab

    def relay_step(step, carry):
        @pl.when(step < views)
        def _():
            view = visit(step)

            @pl.when(step >= 1)
            def _():
                kv_from(view, 0).wait_recv()

            kv_from(view, 1).wait_recv()
            halo(view).start()

        @pl.when((step >= 1) & (step <= views))
        def _():
            view = visit(step + views - 1)
            halo(view).wait_recv()
            cross(view).start()

        @pl.when(step >= LAG)
        def _():
            view = visit(step + views - LAG)

            @pl.when(step > LAG)
            def _():
                q_from(view, 0).wait_recv()

            q_from(view, 1).wait_recv()
            rows = []
            for j in range(2):
                put(j, kv_near[j, view])
                rows.append(bias_row(j * views + view, 1))
            for j in range(2):
                store(j, view, *attend(query(j, view), rows, 2))

        return carry

    lax.fori_loop(0, views + LAG, relay_step, 0)

    hard, easy = upper, 1 - upper

    def near_step(i, carry):
        view = (me + 1 + i) % views
        for j, count, own in ((hard, HARD, False), (easy, EASY, True)):
            rows = []
            if own:
                put(0, kv_near[2 + upper, view])
                rows.append(bias_row((2 + upper) * views + view, 1))
            for n in range(count):
                code = table[2 * view + j, n]
                index, valid = code % VALID, code // VALID
                put(len(rows), kv_near[index // views, index % views])
                rows.append(bias_row(index, valid))
            acc, top = attend(query(j, view), rows, len(rows))
            store(j, view, *merge(j, view, acc, top))
        return carry

    lax.fori_loop(0, views, near_step, 0)

    for step in range(views):
        cross(visit(step)).wait_recv()

    def far_step(i, carry):
        view = (me + 1 + i) % views
        for j, count, own in ((hard, HARD, True), (easy, EASY, False)):
            rows = []
            if own:
                there = jnp.where(upper > 0, jnp.where(base + 2 < bands, 1, 0), jnp.where(base > 0, 1, 0))
                put(0, kv_far[1 - upper, view])
                rows.append(bias_row((5 - upper) * views + view, there))
            for n in range(count, LISTED):
                code = table[2 * view + j, n]
                index, valid = code % VALID, code // VALID
                near_index = jnp.minimum(index, 4 * views - 1)
                far_index = jnp.maximum(index - 4 * views, 0)
                near = kv_near[near_index // views, near_index % views]
                far = kv_far[far_index // views, far_index % views]
                put(len(rows), jnp.where(index < 4 * views, near, far))
                rows.append(bias_row(index, valid))
            acc, top = attend(query(j, view), rows, len(rows))
            total, _ = merge(j, view, acc, top)
            blend = total[:, :cols] / total[:, cols:]
            o_send[j, view] = jnp.where(low_part, turn(blend[:part_rows]), blend[part_rows:]).astype(jnp.bfloat16)

            @pl.when((i < views - 1) | (j != odd))
            def _():
                o_to(view, j).start()

        return carry

    lax.fori_loop(0, views, far_step, 0)
    o_buf[2 * me + head] = o_send[odd, me]
    wo_load.wait()
    for view in others:
        o_from(view, 0).wait_recv()
    for view in [me, *others]:
        o_from(view, 1).wait_recv()

    total = row.astype(jnp.float32)
    for c in range(chips):
        groups = []
        for g in (2 * c, 2 * c + 1):
            a, b = o_buf[2 * g].astype(jnp.float32), o_buf[2 * g + 1].astype(jnp.float32)
            groups.append(
                jnp.concatenate([jnp.where(low_part, a, turn(b)), jnp.where(low_part, turn(a), b)], axis=0)
            )
        both = jnp.concatenate(groups, axis=1).astype(jnp.bfloat16)
        total = total + jnp.dot(both, wo_buf[c * wide : (c + 1) * wide], preferred_element_type=jnp.float32)
    out[...] = total

    for view in others:
        for theirs in range(2):
            kv_to(view, theirs).wait_send()
            q_to(view, theirs).wait_send()
        for j in range(2):
            o_to(view, j).wait_send()
    kv_to(me, 1).wait_send()
    q_to(me, 1).wait_send()
    o_to(me, 1 - odd).wait_send()
    for view in [me, *others]:
        halo(view).wait_send()
        cross(view).wait_send()


def epipolar_table(epipolar_bands, band, views):
    place = band % RING
    base, upper = band - place % 2, place // 2
    listed = lax.dynamic_slice_in_dim(epipolar_bands, base, 2, axis=1)
    numbers = jnp.arange(views, dtype=jnp.int32)
    own = (numbers[:, None] == numbers[None, :])[:, None, :]
    present = (listed >= 0) & ~own
    far = jnp.where(present, listed - base, 0)
    after, before = jnp.where(upper > 0, 2, 1), jnp.where(upper > 0, 1, 2)
    group = jnp.where(far > 1, after, jnp.where(far < 0, before, 0))
    code = (2 * group + (far + 2) % 2) * views + numbers + jnp.where(present, VALID, 0)
    key = jnp.where(own, 3, group) * views + numbers
    rank = jnp.sum((key[:, :, None, :] < key[:, :, :, None]).astype(jnp.int32), axis=3)
    chosen = rank[:, :, :, None] == numbers
    return jnp.sum(jnp.where(chosen, code[:, :, :, None], 0), axis=2).reshape(2 * views, views)


def body(latents, w_qkv, w_out, epipolar_bands, object_token_mask):
    views = lax.axis_size("view")
    bands = lax.axis_size("band")
    tokens, width = latents.shape[1:]
    cols = width // views
    table = epipolar_table(epipolar_bands, lax.axis_index("band"), views)
    bf16, f32 = jnp.bfloat16, jnp.float32
    dma = pltpu.SemaphoreType.DMA
    vmem = pl.BlockSpec(memory_space=pltpu.VMEM)
    hbm = pl.BlockSpec(memory_space=pltpu.HBM)
    updated = pl.pallas_call(
        functools.partial(kernel, views, bands),
        out_shape=jax.ShapeDtypeStruct((tokens, width), f32),
        in_specs=[pl.BlockSpec(memory_space=pltpu.SMEM), vmem, hbm, hbm, hbm],
        out_specs=vmem,
        scratch_shapes=[
            pltpu.VMEM((views // 2, 3, width, 2 * cols), bf16),
            pltpu.VMEM((width, width), bf16),
            pltpu.VMEM((6 * views, tokens), jnp.int32),
            pltpu.VMEM((views, 2, tokens, cols), bf16),
            pltpu.VMEM((views, 2, tokens // 2, cols), bf16),
            pltpu.VMEM((4, views, tokens, cols), bf16),
            pltpu.VMEM((2, views, tokens, cols), bf16),
            pltpu.VMEM((2, views, tokens // 2, cols), bf16),
            pltpu.VMEM(((1 + EASY) * tokens, 2 * cols), bf16),
            pltpu.VMEM((2, views, tokens, 2 * cols), f32),
            pltpu.VMEM((2, views, tokens, cols), f32),
            pltpu.VMEM((2, views, tokens // 2, cols), bf16),
            pltpu.VMEM((2 * views, tokens // 2, cols), bf16),
            dma((views // 2, 3)),
            dma,
            dma((6,)),
            dma((views, 2)),
            dma((2, views)),
            dma((views, 2)),
            dma((2, views)),
            dma((views,)),
            dma((views,)),
            dma((views,)),
            dma((views,)),
            dma((2, views)),
            dma((2 * views,)),
        ],
        compiler_params=pltpu.CompilerParams(
            collective_id=0, has_side_effects=True, vmem_limit_bytes=60 * 2**20
        ),
    )(table, latents[0], w_qkv, w_out, object_token_mask)
    return updated[None]


def solution(mesh):
    placed = (P("view", "band", None), P(), P(), P(), P())
    return jax.shard_map(
        body, mesh=mesh, in_specs=placed, out_specs=P("view", "band", None), check_vma=False
    )
```

```python
import functools
import itertools

import jax
import jax.numpy as jnp
from jax import lax
from jax.experimental import pallas as pl
from jax.experimental.pallas import tpu as pltpu
from jax.sharding import PartitionSpec as P

MESH = pl.DeviceIdType.MESH
HEAD_DIM = 64
RING = 4
LISTED = 7
HARD = 3
EASY = 5
FIRST = 1
AT_ONCE = 1
CATS = 2 * AT_ONCE
BIG = -1e30
VALID = 64


def kernel(
    views, bands, table, lat, w_qkv, w_out, mask, out,
    w_buf, wo_buf, mask_buf, kv_send, q_send, kv_own, kv_side, kv_far, q_buf, *rest,
):
    cats = rest[:CATS]
    (acc_buf, top_buf, o_send, o_buf, w_sem, wo_sem, mask_sem, kv_ssem, kv_rsem, q_ssem, q_rsem, halo_ssem, halo_rsem,
     cross_ssem, cross_rsem, o_ssem, o_rsem) = rest[CATS:]
    tokens, width = lat.shape
    part_rows = tokens // 2
    cols = width // views
    wide = 2 * cols
    chips = views // 2
    me = lax.axis_index("view")
    band = lax.axis_index("band")
    chip, core = me // 2, me % 2
    place = band % RING
    upper, odd = place // 2, place % 2
    head = (odd + upper) % 2
    base = band - odd
    partner = band + 1 - 2 * odd
    across = band + 3 - 2 * place
    over, under = (band + RING) % bands, (band + bands - RING) % bands
    beyond = (band + bands + RING * (1 - 2 * upper)) % bands

    def visit(step):
        near = step // 2 % chips
        return 2 * ((chip + near + near // 2 - 2 * (near // 3)) % chips) + (core + step) % 2

    loads = {}

    def fetch(part, n):
        there = visit(2 * n) // 2
        load = pltpu.make_async_copy(
            w_qkv.at[:, pl.ds(pl.multiple_of(part * width + there * wide, wide), wide)],
            w_buf.at[n, part],
            w_sem.at[n, part],
        )
        load.start()
        loads[n, part] = load

    for n, part in itertools.product(range(chips), (1, 2)):
        fetch(part, n)

    barrier = pltpu.get_barrier_semaphore()
    for off in range(1, views):
        for row in (band, partner):
            pl.semaphore_signal(barrier, 1, device_id=((me + off) % views, row), device_id_type=MESH)
    for row in (partner, across, over, under):
        pl.semaphore_signal(barrier, 1, device_id=(me, row), device_id_type=MESH)

    for n in range(chips):
        fetch(0, n)
    masks = []
    side = 2 - 4 * upper
    for group, shift in enumerate((0, side, -side)):
        for j in range(2):
            at = jnp.clip(base + shift + j, 0, bands - 1)
            load = pltpu.make_async_copy(
                mask.at[:, pl.ds(pl.multiple_of(at * tokens, tokens), tokens)],
                mask_buf.at[pl.ds((2 * group + j) * views, views)],
                mask_sem.at[2 * group + j],
            )
            load.start()
            masks.append(load)
    wo_load = pltpu.make_async_copy(w_out, wo_buf, wo_sem)
    wo_load.start()

    def copy(src, dst, ssem, rsem, view, at):
        return pltpu.make_async_remote_copy(
            src_ref=src, dst_ref=dst, send_sem=ssem, recv_sem=rsem,
            device_id=(view, at), device_id_type=MESH,
        )

    def kv_to(view, theirs):
        h = (head + theirs) % 2
        return copy(
            kv_send.at[view, h], kv_own.at[odd, me], kv_ssem.at[view, h], kv_rsem.at[odd, me],
            view, partner if theirs else band,
        )

    def q_to(view, theirs):
        h = (head + theirs) % 2
        return copy(
            q_send.at[view, h], q_buf.at[odd, me], q_ssem.at[view, h], q_rsem.at[odd, me],
            view, partner if theirs else band,
        )

    def kv_from(view, theirs):
        j = (odd + theirs) % 2
        at = kv_own.at[j, view]
        return copy(at, at, kv_ssem.at[view, 0], kv_rsem.at[j, view], me, partner)

    def q_from(view, theirs):
        j = (odd + theirs) % 2
        at = q_buf.at[j, view]
        return copy(at, at, q_ssem.at[view, 0], q_rsem.at[j, view], me, partner)

    def halo(view):
        return copy(
            kv_own.at[pl.ds(0, 2), view], kv_side.at[pl.ds(0, 2), view], halo_ssem.at[view], halo_rsem.at[view],
            me, across,
        )

    def cross(view):
        return copy(
            kv_side.at[pl.ds(0, 2), view], kv_far.at[pl.ds(0, 2), view], cross_ssem.at[view], cross_rsem.at[view],
            me, beyond,
        )

    def o_to(view, j):
        return copy(
            o_send.at[j, view], o_buf.at[2 * me + head], o_ssem.at[j, view], o_rsem.at[2 * me + head], view, base + j
        )

    def o_from(view, theirs):
        slot = 2 * view + (head + theirs) % 2
        at = o_buf.at[slot]
        return copy(at, at, o_ssem.at[0, view], o_rsem.at[slot], me, partner)

    row = lat[...]
    scale = HEAD_DIM**-0.5
    low = lax.broadcasted_iota(jnp.int32, (tokens, cols), 1) < HEAD_DIM
    low_part = lax.broadcasted_iota(jnp.int32, (part_rows, cols), 1) < HEAD_DIM

    def turn(x):
        return pltpu.roll(x, HEAD_DIM, 1)

    def project(n, part):
        loads[n, part].wait()
        return jnp.dot(row, w_buf[n, part], preferred_element_type=jnp.float32)

    others = [visit(step) for step in range(1, views)]

    for n in range(chips):
        there = visit(2 * n) // 2
        keys, values = project(n, 1), project(n, 2)
        for c in range(2):
            k = keys[:, c * cols : (c + 1) * cols]
            v = values[:, c * cols : (c + 1) * cols]
            kv_send[2 * there + c, 0] = jnp.where(low, k, turn(v)).astype(jnp.bfloat16)
            kv_send[2 * there + c, 1] = jnp.where(low, turn(k), v).astype(jnp.bfloat16)
        if n == 0:
            kv_own[odd, me] = kv_send[me, head]
            pl.semaphore_wait(barrier, 2 * views + 2)
            kv_to(me, 1).start()
            for theirs in range(2):
                kv_to(2 * chip + 1 - core, theirs).start()
        else:
            for c, theirs in itertools.product(range(2), range(2)):
                kv_to(2 * there + c, theirs).start()
    for n in range(chips):
        there = visit(2 * n) // 2
        queries = project(n, 0) * scale
        for c in range(2):
            first = queries[:part_rows, c * cols : (c + 1) * cols]
            second = queries[part_rows:, c * cols : (c + 1) * cols]
            q_send[2 * there + c, 0] = jnp.where(low_part, first, turn(second)).astype(jnp.bfloat16)
            q_send[2 * there + c, 1] = jnp.where(low_part, turn(first), second).astype(jnp.bfloat16)
        if n == 0:
            q_buf[odd, me] = q_send[me, head]
            q_to(me, 1).start()
            for theirs in range(2):
                q_to(2 * chip + 1 - core, theirs).start()
        else:
            for c, theirs in itertools.product(range(2), range(2)):
                q_to(2 * there + c, theirs).start()

    for load in masks:
        load.wait()
    for cat in cats:
        cat[:, cols:] = jnp.ones((cat.shape[0], cols), jnp.bfloat16)

    def bias_row(index, valid):
        seen = mask_buf[pl.ds(index, 1), :] * valid
        return jnp.where(seen > 0, 0.0, BIG)

    def query(j, view):
        both = q_buf[j, view].astype(jnp.float32)
        rows = jnp.concatenate([jnp.where(low_part, both, 0.0), jnp.where(low_part, turn(both), 0.0)], axis=0)
        return rows.astype(jnp.bfloat16)

    def attend(cat, q, rows, count):
        keys = count * tokens
        s = lax.dot_general(
            q, cat[:keys, :cols], (((1,), (1,)), ((), ())), preferred_element_type=jnp.float32
        )
        s = s + jnp.concatenate(rows, axis=1)
        top = jnp.max(s, axis=1, keepdims=True)
        p = jnp.exp(s - top).astype(jnp.bfloat16)
        return jnp.dot(p, cat[:keys], preferred_element_type=jnp.float32), top

    def store(j, view, acc, top):
        acc_buf[j, view] = acc
        top_buf[j, view] = jnp.broadcast_to(top, (tokens, cols))

    def merge(j, view, acc, top):
        old = top_buf[j, view][:, :1]
        new = jnp.maximum(old, top)
        return acc_buf[j, view] * jnp.exp(old - new) + acc * jnp.exp(top - new), new

    hard, easy = upper, 1 - upper

    def gather(cat, spots, listed, held):
        rows = []
        for slab, index, valid in spots:
            cat[len(rows) * tokens : (len(rows) + 1) * tokens, :cols] = slab
            rows.append(bias_row(index, valid))
        for code in listed:
            index, valid = code % VALID, code // VALID
            pick, view = index // views, index % views
            slab = held[0][pick % 2, view]
            for group in range(1, len(held)):
                slab = jnp.where(pick // 2 == group, held[group][pick % 2, view], slab)
            cat[len(rows) * tokens : (len(rows) + 1) * tokens, :cols] = slab
            rows.append(bias_row(index, valid))
        return rows

    def relay_step(step, carry):
        view = visit(step)

        @pl.when(step >= 1)
        def _():
            kv_from(view, 0).wait_recv()

        kv_from(view, 1).wait_recv()
        halo(view).start()
        return carry

    lax.fori_loop(0, views, relay_step, 0)

    def own_step(step, carry):
        view = visit(step)
        halo(view).wait_recv()
        cross(view).start()

        @pl.when(step >= 1)
        def _():
            q_from(view, 0).wait_recv()

        q_from(view, 1).wait_recv()
        for n, j in enumerate((hard, easy)):
            spots = [(kv_own[0, view], view, 1), (kv_own[1, view], views + view, 1)]
            if n == 1:
                spots.append((kv_side[upper, view], (2 + upper) * views + view, 1))
            rows = gather(cats[n], spots, [table[2 * view + j, r] for r in range(FIRST)], (kv_own,))
            store(j, view, *attend(cats[n], query(j, view), rows, len(rows)))
        return carry

    lax.fori_loop(0, views, own_step, 0)

    def near_step(i, carry):
        for turn_ in range(AT_ONCE):
            view = (me + 1 + AT_ONCE * i + turn_) % views
            for n, (j, count) in enumerate(((hard, HARD), (easy, EASY))):
                cat = cats[2 * turn_ + n]
                rows = gather(cat, [], [table[2 * view + j, r] for r in range(FIRST, count)], (kv_own, kv_side))
                acc, top = attend(cat, query(j, view), rows, len(rows))
                store(j, view, *merge(j, view, acc, top))
        return carry

    lax.fori_loop(0, views // AT_ONCE, near_step, 0)

    for step in range(views):
        cross(visit(step)).wait_recv()

    def far_step(i, carry):
        for turn_ in range(AT_ONCE):
            view = (me + 1 + AT_ONCE * i + turn_) % views
            for n, (j, count) in enumerate(((hard, HARD), (easy, EASY))):
                cat = cats[2 * turn_ + n]
                spots = []
                if n == 0:
                    there = jnp.where(upper > 0, jnp.where(base + 2 < bands, 1, 0), jnp.where(base > 0, 1, 0))
                    spots.append((kv_far[1 - upper, view], (5 - upper) * views + view, there))
                listed = [table[2 * view + j, r] for r in range(count, LISTED)]
                rows = gather(cat, spots, listed, (kv_own, kv_side, kv_far))
                acc, top = attend(cat, query(j, view), rows, len(rows))
                total, _ = merge(j, view, acc, top)
                blend = total[:, :cols] / total[:, cols:]
                packed = jnp.where(low_part, turn(blend[:part_rows]), blend[part_rows:])
                o_send[j, view] = packed.astype(jnp.bfloat16)
        for turn_ in range(AT_ONCE):
            nth = AT_ONCE * i + turn_
            view = (me + 1 + nth) % views
            o_to(view, 1 - odd).start()

            @pl.when(nth < views - 1)
            def _():
                o_to(view, odd).start()

        return carry

    lax.fori_loop(0, views // AT_ONCE, far_step, 0)
    o_buf[2 * me + head] = o_send[odd, me]
    wo_load.wait()
    for view in others:
        o_from(view, 0).wait_recv()
    for view in [me, *others]:
        o_from(view, 1).wait_recv()

    total = row.astype(jnp.float32)
    for c in range(chips):
        groups = []
        for g in (2 * c, 2 * c + 1):
            a, b = o_buf[2 * g].astype(jnp.float32), o_buf[2 * g + 1].astype(jnp.float32)
            groups.append(
                jnp.concatenate([jnp.where(low_part, a, turn(b)), jnp.where(low_part, turn(a), b)], axis=0)
            )
        both = jnp.concatenate(groups, axis=1).astype(jnp.bfloat16)
        total = total + jnp.dot(both, wo_buf[c * wide : (c + 1) * wide], preferred_element_type=jnp.float32)
    out[...] = total

    for view in others:
        for theirs in range(2):
            kv_to(view, theirs).wait_send()
            q_to(view, theirs).wait_send()
        for j in range(2):
            o_to(view, j).wait_send()
    kv_to(me, 1).wait_send()
    q_to(me, 1).wait_send()
    o_to(me, 1 - odd).wait_send()
    for view in [me, *others]:
        halo(view).wait_send()
        cross(view).wait_send()


def epipolar_table(epipolar_bands, band, views):
    place = band % RING
    base, upper = band - place % 2, place // 2
    listed = lax.dynamic_slice_in_dim(epipolar_bands, base, 2, axis=1)
    numbers = jnp.arange(views, dtype=jnp.int32)
    own = (numbers[:, None] == numbers[None, :])[:, None, :]
    present = (listed >= 0) & ~own
    far = jnp.where(present, listed - base, 0)
    after, before = jnp.where(upper > 0, 2, 1), jnp.where(upper > 0, 1, 2)
    group = jnp.where(far > 1, after, jnp.where(far < 0, before, 0))
    code = (2 * group + (far + 2) % 2) * views + numbers + jnp.where(present, VALID, 0)
    key = jnp.where(own, 3, group) * views + numbers
    rank = jnp.sum((key[:, :, None, :] < key[:, :, :, None]).astype(jnp.int32), axis=3)
    chosen = rank[:, :, :, None] == numbers
    return jnp.sum(jnp.where(chosen, code[:, :, :, None], 0), axis=2).reshape(2 * views, views)


def body(latents, w_qkv, w_out, epipolar_bands, object_token_mask):
    views = lax.axis_size("view")
    bands = lax.axis_size("band")
    tokens, width = latents.shape[1:]
    cols = width // views
    table = epipolar_table(epipolar_bands, lax.axis_index("band"), views)
    bf16, f32 = jnp.bfloat16, jnp.float32
    dma = pltpu.SemaphoreType.DMA
    vmem = pl.BlockSpec(memory_space=pltpu.VMEM)
    hbm = pl.BlockSpec(memory_space=pltpu.HBM)
    updated = pl.pallas_call(
        functools.partial(kernel, views, bands),
        out_shape=jax.ShapeDtypeStruct((tokens, width), f32),
        in_specs=[pl.BlockSpec(memory_space=pltpu.SMEM), vmem, hbm, hbm, hbm],
        out_specs=vmem,
        scratch_shapes=[
            pltpu.VMEM((views // 2, 3, width, 2 * cols), bf16),
            pltpu.VMEM((width, width), bf16),
            pltpu.VMEM((6 * views, tokens), jnp.int32),
            pltpu.VMEM((views, 2, tokens, cols), bf16),
            pltpu.VMEM((views, 2, tokens // 2, cols), bf16),
            *[pltpu.VMEM((2, views, tokens, cols), bf16) for _ in range(3)],
            pltpu.VMEM((2, views, tokens // 2, cols), bf16),
            *[pltpu.VMEM(((LISTED - 1) * tokens, 2 * cols), bf16) for _ in range(CATS)],
            pltpu.VMEM((2, views, tokens, 2 * cols), f32),
            pltpu.VMEM((2, views, tokens, cols), f32),
            pltpu.VMEM((2, views, tokens // 2, cols), bf16),
            pltpu.VMEM((2 * views, tokens // 2, cols), bf16),
            dma((views // 2, 3)),
            dma,
            dma((6,)),
            dma((views, 2)),
            dma((2, views)),
            dma((views, 2)),
            dma((2, views)),
            dma((views,)),
            dma((views,)),
            dma((views,)),
            dma((views,)),
            dma((2, views)),
            dma((2 * views,)),
        ],
        compiler_params=pltpu.CompilerParams(
            collective_id=0, has_side_effects=True, vmem_limit_bytes=60 * 2**20
        ),
    )(table, latents[0], w_qkv, w_out, object_token_mask)
    return updated[None]


def solution(mesh):
    placed = (P("view", "band", None), P(), P(), P(), P())
    return jax.shard_map(
        body, mesh=mesh, in_specs=placed, out_specs=P("view", "band", None), check_vma=False
    )
```

```python
import functools
import itertools

import jax
import jax.numpy as jnp
from jax import lax
from jax.experimental import pallas as pl
from jax.experimental.pallas import tpu as pltpu
from jax.sharding import PartitionSpec as P

MESH = pl.DeviceIdType.MESH
HEAD_DIM = 64
RING = 4
LISTED = 7
HARD = 3
EASY = 5
FIRST = 1
AT_ONCE = 1
CATS = 2 * AT_ONCE
BIG = -1e30
VALID = 64


def kernel(
    views, bands, listing, lat_hbm, w_qkv, mask, out,
    table, lat, w_buf, mask_buf, kv_send, q_send, kv_own, kv_side, kv_far, q_buf, *rest,
):
    cats = rest[:CATS]
    (acc_buf, top_buf, o_send, o_buf, lat_sem, w_sem, mask_sem, kv_ssem, kv_rsem, q_ssem, q_rsem, halo_ssem, halo_rsem,
     cross_ssem, cross_rsem, o_ssem, o_rsem) = rest[CATS:]
    tokens, width = lat.shape
    lat_load = pltpu.make_async_copy(lat_hbm, lat, lat_sem)
    lat_load.start()
    part_rows = tokens // 2
    cols = width // views
    wide = 2 * cols
    chips = views // 2
    me = lax.axis_index("view")
    band = lax.axis_index("band")
    chip, core = me // 2, me % 2
    place = band % RING
    upper, odd = place // 2, place % 2
    head = (odd + upper) % 2
    base = band - odd
    partner = band + 1 - 2 * odd
    across = band + 3 - 2 * place
    over, under = (band + RING) % bands, (band + bands - RING) % bands
    beyond = (band + bands + RING * (1 - 2 * upper)) % bands

    def visit(step):
        near = step // 2 % chips
        return 2 * ((chip + near + near // 2 - 2 * (near // 3)) % chips) + (core + step) % 2

    loads = {}

    def fetch(part, n):
        there = visit(2 * n) // 2
        load = pltpu.make_async_copy(
            w_qkv.at[:, pl.ds(pl.multiple_of(part * width + there * wide, wide), wide)],
            w_buf.at[n, part],
            w_sem.at[n, part],
        )
        load.start()
        loads[n, part] = load

    for n, part in itertools.product(range(chips), (1, 2)):
        fetch(part, n)

    barrier = pltpu.get_barrier_semaphore()
    for off in range(1, views):
        for row in (band, partner):
            pl.semaphore_signal(barrier, 1, device_id=((me + off) % views, row), device_id_type=MESH)
    for row in (partner, across, over, under):
        pl.semaphore_signal(barrier, 1, device_id=(me, row), device_id_type=MESH)

    for n in range(chips):
        fetch(0, n)
    masks = []
    side = 2 - 4 * upper
    for group, shift in enumerate((0, side, -side)):
        for j in range(2):
            at = jnp.clip(base + shift + j, 0, bands - 1)
            load = pltpu.make_async_copy(
                mask.at[:, pl.ds(pl.multiple_of(at * tokens, tokens), tokens)],
                mask_buf.at[pl.ds((2 * group + j) * views, views)],
                mask_sem.at[2 * group + j],
            )
            load.start()
            masks.append(load)

    def copy(src, dst, ssem, rsem, view, at):
        return pltpu.make_async_remote_copy(
            src_ref=src, dst_ref=dst, send_sem=ssem, recv_sem=rsem,
            device_id=(view, at), device_id_type=MESH,
        )

    def kv_to(view, theirs):
        h = (head + theirs) % 2
        return copy(
            kv_send.at[view, h], kv_own.at[odd, me], kv_ssem.at[view, h], kv_rsem.at[odd, me],
            view, partner if theirs else band,
        )

    def q_to(view, theirs):
        h = (head + theirs) % 2
        return copy(
            q_send.at[view, h], q_buf.at[odd, me], q_ssem.at[view, h], q_rsem.at[odd, me],
            view, partner if theirs else band,
        )

    def kv_from(view, theirs):
        j = (odd + theirs) % 2
        at = kv_own.at[j, view]
        return copy(at, at, kv_ssem.at[view, 0], kv_rsem.at[j, view], me, partner)

    def q_from(view, theirs):
        j = (odd + theirs) % 2
        at = q_buf.at[j, view]
        return copy(at, at, q_ssem.at[view, 0], q_rsem.at[j, view], me, partner)

    def halo(view):
        return copy(
            kv_own.at[pl.ds(0, 2), view], kv_side.at[pl.ds(0, 2), view], halo_ssem.at[view], halo_rsem.at[view],
            me, across,
        )

    def cross(view):
        return copy(
            kv_side.at[pl.ds(0, 2), view], kv_far.at[pl.ds(0, 2), view], cross_ssem.at[view], cross_rsem.at[view],
            me, beyond,
        )

    def o_to(view, j):
        return copy(
            o_send.at[j, view], o_buf.at[2 * me + head], o_ssem.at[j, view], o_rsem.at[2 * me + head], view, base + j
        )

    def o_from(view, theirs):
        slot = 2 * view + (head + theirs) % 2
        at = o_buf.at[slot]
        return copy(at, at, o_ssem.at[0, view], o_rsem.at[slot], me, partner)

    lat_load.wait()
    row = lat[...]
    scale = HEAD_DIM**-0.5
    low = lax.broadcasted_iota(jnp.int32, (tokens, cols), 1) < HEAD_DIM
    low_part = lax.broadcasted_iota(jnp.int32, (part_rows, cols), 1) < HEAD_DIM

    def turn(x):
        return pltpu.roll(x, HEAD_DIM, 1)

    def project(n, part):
        loads[n, part].wait()
        return jnp.dot(row, w_buf[n, part], preferred_element_type=jnp.float32)

    others = [visit(step) for step in range(1, views)]

    for n in range(chips):
        there = visit(2 * n) // 2
        keys, values = project(n, 1), project(n, 2)
        for c in range(2):
            k = keys[:, c * cols : (c + 1) * cols]
            v = values[:, c * cols : (c + 1) * cols]
            kv_send[2 * there + c, 0] = jnp.where(low, k, turn(v)).astype(jnp.bfloat16)
            kv_send[2 * there + c, 1] = jnp.where(low, turn(k), v).astype(jnp.bfloat16)
        if n == 0:
            kv_own[odd, me] = kv_send[me, head]
            pl.semaphore_wait(barrier, 2 * views + 2)
            kv_to(me, 1).start()
            for theirs in range(2):
                kv_to(2 * chip + 1 - core, theirs).start()
        else:
            for c, theirs in itertools.product(range(2), range(2)):
                kv_to(2 * there + c, theirs).start()
    for n in range(chips):
        there = visit(2 * n) // 2
        queries = project(n, 0) * scale
        for c in range(2):
            first = queries[:part_rows, c * cols : (c + 1) * cols]
            second = queries[part_rows:, c * cols : (c + 1) * cols]
            q_send[2 * there + c, 0] = jnp.where(low_part, first, turn(second)).astype(jnp.bfloat16)
            q_send[2 * there + c, 1] = jnp.where(low_part, turn(first), second).astype(jnp.bfloat16)
        if n == 0:
            q_buf[odd, me] = q_send[me, head]
            q_to(me, 1).start()
            for theirs in range(2):
                q_to(2 * chip + 1 - core, theirs).start()
        else:
            for c, theirs in itertools.product(range(2), range(2)):
                q_to(2 * there + c, theirs).start()

    for load in masks:
        load.wait()
    for cat in cats:
        cat[:, cols:] = jnp.ones((cat.shape[0], cols), jnp.bfloat16)

    def bias_row(index, valid):
        seen = mask_buf[pl.ds(index, 1), :] * valid
        return jnp.where(seen > 0, 0.0, BIG)

    def query(j, view):
        both = q_buf[j, view].astype(jnp.float32)
        rows = jnp.concatenate([jnp.where(low_part, both, 0.0), jnp.where(low_part, turn(both), 0.0)], axis=0)
        return rows.astype(jnp.bfloat16)

    def attend(cat, q, rows, count):
        keys = count * tokens
        s = lax.dot_general(
            q, cat[:keys, :cols], (((1,), (1,)), ((), ())), preferred_element_type=jnp.float32
        )
        s = s + jnp.concatenate(rows, axis=1)
        top = jnp.max(s, axis=1, keepdims=True)
        p = jnp.exp(s - top).astype(jnp.bfloat16)
        return jnp.dot(p, cat[:keys], preferred_element_type=jnp.float32), top

    def store(j, view, acc, top):
        acc_buf[j, view] = acc
        top_buf[j, view] = jnp.broadcast_to(top, (tokens, cols))

    def merge(j, view, acc, top):
        old = top_buf[j, view][:, :1]
        new = jnp.maximum(old, top)
        return acc_buf[j, view] * jnp.exp(old - new) + acc * jnp.exp(top - new), new

    hard, easy = upper, 1 - upper

    def gather(cat, spots, listed, held):
        rows = []
        for slab, index, valid in spots:
            cat[len(rows) * tokens : (len(rows) + 1) * tokens, :cols] = slab
            rows.append(bias_row(index, valid))
        for code in listed:
            index, valid = code % VALID, code // VALID
            pick, view = index // views, index % views
            slab = held[0][pick % 2, view]
            for group in range(1, len(held)):
                slab = jnp.where(pick // 2 == group, held[group][pick % 2, view], slab)
            cat[len(rows) * tokens : (len(rows) + 1) * tokens, :cols] = slab
            rows.append(bias_row(index, valid))
        return rows

    def order_list(n):
        query_view, j = n // 2, n % 2
        codes, keys = [], []
        for off in range(1, views):
            view = (query_view + off) % views
            listed = listing[query_view, view, base + j]
            present = jnp.where(listed >= 0, 1, 0)
            far = present * (listed - base)
            after, before = jnp.where(far > 1, 1, 0), jnp.where(far < 0, 1, 0)
            group = (1 + upper) * after + (2 - upper) * before
            second = jnp.where((far == 1) | (far == 3) | (far == -1), 1, 0)
            codes.append((2 * group + second) * views + view + VALID * present)
            keys.append(group * views + off)
        ranks = []
        for a in keys:
            ranks.append(sum(jnp.where(b < a, 1, 0) for b in keys if b is not a))
        for place_ in range(LISTED):
            table[n, place_] = sum(jnp.where(r == place_, c, 0) for r, c in zip(ranks, codes))

    def relay_step(step, carry):
        view = visit(step)

        @pl.when(step >= 1)
        def _():
            kv_from(view, 0).wait_recv()

        kv_from(view, 1).wait_recv()
        halo(view).start()
        for j in range(2):
            order_list(2 * step + j)
        return carry

    lax.fori_loop(0, views, relay_step, 0)

    def own_step(step, carry):
        view = visit(step)
        halo(view).wait_recv()
        cross(view).start()

        @pl.when(step >= 1)
        def _():
            q_from(view, 0).wait_recv()

        q_from(view, 1).wait_recv()
        for n, j in enumerate((hard, easy)):
            spots = [(kv_own[0, view], view, 1), (kv_own[1, view], views + view, 1)]
            if n == 1:
                spots.append((kv_side[upper, view], (2 + upper) * views + view, 1))
            rows = gather(cats[n], spots, [table[2 * view + j, r] for r in range(FIRST)], (kv_own,))
            store(j, view, *attend(cats[n], query(j, view), rows, len(rows)))
        return carry

    lax.fori_loop(0, views, own_step, 0)

    def near_step(i, carry):
        for turn_ in range(AT_ONCE):
            view = (me + 1 + AT_ONCE * i + turn_) % views
            for n, (j, count) in enumerate(((hard, HARD), (easy, EASY))):
                cat = cats[2 * turn_ + n]
                rows = gather(cat, [], [table[2 * view + j, r] for r in range(FIRST, count)], (kv_own, kv_side))
                acc, top = attend(cat, query(j, view), rows, len(rows))
                store(j, view, *merge(j, view, acc, top))
        return carry

    lax.fori_loop(0, views // AT_ONCE, near_step, 0)

    for step in range(views):
        cross(visit(step)).wait_recv()

    def far_step(i, carry):
        for turn_ in range(AT_ONCE):
            view = (me + 1 + AT_ONCE * i + turn_) % views
            for n, (j, count) in enumerate(((hard, HARD), (easy, EASY))):
                cat = cats[2 * turn_ + n]
                spots = []
                if n == 0:
                    there = jnp.where(upper > 0, jnp.where(base + 2 < bands, 1, 0), jnp.where(base > 0, 1, 0))
                    spots.append((kv_far[1 - upper, view], (5 - upper) * views + view, there))
                listed = [table[2 * view + j, r] for r in range(count, LISTED)]
                rows = gather(cat, spots, listed, (kv_own, kv_side, kv_far))
                acc, top = attend(cat, query(j, view), rows, len(rows))
                total, _ = merge(j, view, acc, top)
                blend = total[:, :cols] / total[:, cols:]
                packed = jnp.where(low_part, turn(blend[:part_rows]), blend[part_rows:])
                o_send[j, view] = packed.astype(jnp.bfloat16)
        for turn_ in range(AT_ONCE):
            nth = AT_ONCE * i + turn_
            view = (me + 1 + nth) % views
            o_to(view, 1 - odd).start()

            @pl.when(nth < views - 1)
            def _():
                o_to(view, odd).start()

        return carry

    lax.fori_loop(0, views // AT_ONCE, far_step, 0)
    o_buf[2 * me + head] = o_send[odd, me]
    for view in others:
        o_from(view, 0).wait_recv()
    for view in [me, *others]:
        o_from(view, 1).wait_recv()

    for g in range(views):
        a, b = o_buf[2 * g].astype(jnp.float32), o_buf[2 * g + 1].astype(jnp.float32)
        both = jnp.concatenate([jnp.where(low_part, a, turn(b)), jnp.where(low_part, turn(a), b)], axis=0)
        out[:, g * cols : (g + 1) * cols] = both.astype(jnp.bfloat16)

    for view in others:
        for theirs in range(2):
            kv_to(view, theirs).wait_send()
            q_to(view, theirs).wait_send()
        for j in range(2):
            o_to(view, j).wait_send()
    kv_to(me, 1).wait_send()
    q_to(me, 1).wait_send()
    o_to(me, 1 - odd).wait_send()
    for view in [me, *others]:
        halo(view).wait_send()
        cross(view).wait_send()


def body(latents, w_qkv, w_out, epipolar_bands, object_token_mask):
    views = lax.axis_size("view")
    bands = lax.axis_size("band")
    tokens, width = latents.shape[1:]
    cols = width // views
    bf16, f32 = jnp.bfloat16, jnp.float32
    dma = pltpu.SemaphoreType.DMA
    vmem = pl.BlockSpec(memory_space=pltpu.VMEM)
    hbm = pl.BlockSpec(memory_space=pltpu.HBM)
    blended = pl.pallas_call(
        functools.partial(kernel, views, bands),
        out_shape=jax.ShapeDtypeStruct((tokens, width), bf16),
        in_specs=[pl.BlockSpec(memory_space=pltpu.SMEM), hbm, hbm, hbm],
        out_specs=vmem,
        scratch_shapes=[
            pltpu.SMEM((2 * views, LISTED), jnp.int32),
            pltpu.VMEM((tokens, width), bf16),
            pltpu.VMEM((views // 2, 3, width, 2 * cols), bf16),
            pltpu.VMEM((6 * views, tokens), jnp.int32),
            pltpu.VMEM((views, 2, tokens, cols), bf16),
            pltpu.VMEM((views, 2, tokens // 2, cols), bf16),
            *[pltpu.VMEM((2, views, tokens, cols), bf16) for _ in range(3)],
            pltpu.VMEM((2, views, tokens // 2, cols), bf16),
            *[pltpu.VMEM(((LISTED - 1) * tokens, 2 * cols), bf16) for _ in range(CATS)],
            pltpu.VMEM((2, views, tokens, 2 * cols), f32),
            pltpu.VMEM((2, views, tokens, cols), f32),
            pltpu.VMEM((2, views, tokens // 2, cols), bf16),
            pltpu.VMEM((2 * views, tokens // 2, cols), bf16),
            dma,
            dma((views // 2, 3)),
            dma((6,)),
            dma((views, 2)),
            dma((2, views)),
            dma((views, 2)),
            dma((2, views)),
            dma((views,)),
            dma((views,)),
            dma((views,)),
            dma((views,)),
            dma((2, views)),
            dma((2 * views,)),
        ],
        compiler_params=pltpu.CompilerParams(
            collective_id=0, has_side_effects=True, vmem_limit_bytes=60 * 2**20
        ),
    )(epipolar_bands.transpose(0, 2, 1), latents[0], w_qkv, object_token_mask)
    updated = latents[0].astype(f32) + jnp.dot(blended, w_out, preferred_element_type=f32)
    return updated[None]


def solution(mesh):
    placed = (P("view", "band", None), P(), P(), P(), P())
    return jax.shard_map(
        body, mesh=mesh, in_specs=placed, out_specs=P("view", "band", None), check_vma=False
    )
```

```python
import functools
import itertools

import jax
import jax.numpy as jnp
from jax import lax
from jax.experimental import pallas as pl
from jax.experimental.pallas import tpu as pltpu
from jax.sharding import PartitionSpec as P

MESH = pl.DeviceIdType.MESH
HEAD_DIM = 64
RING = 4
LISTED = 7
HARD = 3
EASY = 5
FIRST = 1
AT_ONCE = 1
CATS = 2 * AT_ONCE
BIG = -1e30
VALID = 64


def kernel(
    views, bands, listing, lat_hbm, w_qkv, mask, out,
    table, lat, w_buf, mask_buf, kv_send, q_send, kv_own, kv_side, kv_far, q_buf, *rest,
):
    cats = rest[:CATS]
    (acc_buf, top_buf, o_send, o_buf, lat_sem, w_sem, mask_sem, kv_ssem, kv_rsem, q_ssem, q_rsem, halo_ssem, halo_rsem,
     cross_ssem, cross_rsem, o_ssem, o_rsem) = rest[CATS:]
    tokens, width = lat.shape
    lat_load = pltpu.make_async_copy(lat_hbm, lat, lat_sem)
    lat_load.start()
    part_rows = tokens // 2
    cols = width // views
    wide = 2 * cols
    chips = views // 2
    me = lax.axis_index("view")
    band = lax.axis_index("band")
    chip, core = me // 2, me % 2
    place = band % RING
    upper, odd = place // 2, place % 2
    head = (odd + upper) % 2
    base = band - odd
    partner = band + 1 - 2 * odd
    across = band + 3 - 2 * place
    over, under = (band + RING) % bands, (band + bands - RING) % bands
    beyond = (band + bands + RING * (1 - 2 * upper)) % bands

    def visit(step):
        near = step // 2 % chips
        return 2 * ((chip + near + near // 2 - 2 * (near // 3)) % chips) + (core + step) % 2

    loads = {}

    def fetch(part, n):
        there = visit(2 * n) // 2
        load = pltpu.make_async_copy(
            w_qkv.at[:, pl.ds(pl.multiple_of(part * width + there * wide, wide), wide)],
            w_buf.at[n, part],
            w_sem.at[n, part],
        )
        load.start()
        loads[n, part] = load

    for n, part in itertools.product(range(chips), (1, 2)):
        fetch(part, n)

    barrier = pltpu.get_barrier_semaphore()
    for off in range(1, views):
        for row in (band, partner):
            pl.semaphore_signal(barrier, 1, device_id=((me + off) % views, row), device_id_type=MESH)
    for row in (partner, across, over, under):
        pl.semaphore_signal(barrier, 1, device_id=(me, row), device_id_type=MESH)

    for n in range(chips):
        fetch(0, n)
    masks = []
    side = 2 - 4 * upper
    for group, shift in enumerate((0, side, -side)):
        for j in range(2):
            at = jnp.clip(base + shift + j, 0, bands - 1)
            load = pltpu.make_async_copy(
                mask.at[:, pl.ds(pl.multiple_of(at * tokens, tokens), tokens)],
                mask_buf.at[pl.ds((2 * group + j) * views, views)],
                mask_sem.at[2 * group + j],
            )
            load.start()
            masks.append(load)

    def copy(src, dst, ssem, rsem, view, at):
        return pltpu.make_async_remote_copy(
            src_ref=src, dst_ref=dst, send_sem=ssem, recv_sem=rsem,
            device_id=(view, at), device_id_type=MESH,
        )

    def kv_to(view, theirs):
        h = (head + theirs) % 2
        return copy(
            kv_send.at[view, h], kv_own.at[odd, me], kv_ssem.at[view, h], kv_rsem.at[odd, me],
            view, partner if theirs else band,
        )

    def q_to(view, theirs):
        h = (head + theirs) % 2
        return copy(
            q_send.at[view, h], q_buf.at[odd, me], q_ssem.at[view, h], q_rsem.at[odd, me],
            view, partner if theirs else band,
        )

    def kv_from(view, theirs):
        j = (odd + theirs) % 2
        at = kv_own.at[j, view]
        return copy(at, at, kv_ssem.at[view, 0], kv_rsem.at[j, view], me, partner)

    def q_from(view, theirs):
        j = (odd + theirs) % 2
        at = q_buf.at[j, view]
        return copy(at, at, q_ssem.at[view, 0], q_rsem.at[j, view], me, partner)

    def halo(view):
        return copy(
            kv_own.at[pl.ds(0, 2), view], kv_side.at[pl.ds(0, 2), view], halo_ssem.at[view], halo_rsem.at[view],
            me, across,
        )

    def cross(view):
        return copy(
            kv_side.at[pl.ds(0, 2), view], kv_far.at[pl.ds(0, 2), view], cross_ssem.at[view], cross_rsem.at[view],
            me, beyond,
        )

    def o_to(view, j):
        return copy(
            o_send.at[j, view], o_buf.at[2 * me + head], o_ssem.at[j, view], o_rsem.at[2 * me + head], view, base + j
        )

    def o_from(view, theirs):
        slot = 2 * view + (head + theirs) % 2
        at = o_buf.at[slot]
        return copy(at, at, o_ssem.at[0, view], o_rsem.at[slot], me, partner)

    lat_load.wait()
    row = lat[...]
    scale = HEAD_DIM**-0.5
    low = lax.broadcasted_iota(jnp.int32, (tokens, cols), 1) < HEAD_DIM
    low_part = lax.broadcasted_iota(jnp.int32, (part_rows, cols), 1) < HEAD_DIM

    def turn(x):
        return pltpu.roll(x, HEAD_DIM, 1)

    def project(n, part):
        loads[n, part].wait()
        return jnp.dot(row, w_buf[n, part], preferred_element_type=jnp.float32)

    others = [visit(step) for step in range(1, views)]

    for n in range(chips):
        there = visit(2 * n) // 2
        keys, values = project(n, 1), project(n, 2)
        for c in range(2):
            k = keys[:, c * cols : (c + 1) * cols]
            v = values[:, c * cols : (c + 1) * cols]
            kv_send[2 * there + c, 0] = jnp.where(low, k, turn(v)).astype(jnp.bfloat16)
            kv_send[2 * there + c, 1] = jnp.where(low, turn(k), v).astype(jnp.bfloat16)
        if n == 0:
            kv_own[odd, me] = kv_send[me, head]
            pl.semaphore_wait(barrier, 2 * views + 2)
            kv_to(me, 1).start()
            for theirs in range(2):
                kv_to(2 * chip + 1 - core, theirs).start()
        else:
            for c, theirs in itertools.product(range(2), range(2)):
                kv_to(2 * there + c, theirs).start()
    for n in range(chips):
        there = visit(2 * n) // 2
        queries = project(n, 0) * scale
        for c in range(2):
            first = queries[:part_rows, c * cols : (c + 1) * cols]
            second = queries[part_rows:, c * cols : (c + 1) * cols]
            q_send[2 * there + c, 0] = jnp.where(low_part, first, turn(second)).astype(jnp.bfloat16)
            q_send[2 * there + c, 1] = jnp.where(low_part, turn(first), second).astype(jnp.bfloat16)
        if n == 0:
            q_buf[odd, me] = q_send[me, head]
            q_to(me, 1).start()
            for theirs in range(2):
                q_to(2 * chip + 1 - core, theirs).start()
        else:
            for c, theirs in itertools.product(range(2), range(2)):
                q_to(2 * there + c, theirs).start()

    for load in masks:
        load.wait()
    for cat in cats:
        cat[:, cols:] = jnp.ones((cat.shape[0], cols), jnp.bfloat16)

    def bias_row(index, valid):
        seen = mask_buf[pl.ds(index, 1), :] * valid
        return jnp.where(seen > 0, 0.0, BIG)

    def query(j, view):
        both = q_buf[j, view].astype(jnp.float32)
        rows = jnp.concatenate([jnp.where(low_part, both, 0.0), jnp.where(low_part, turn(both), 0.0)], axis=0)
        return rows.astype(jnp.bfloat16)

    def attend(cat, q, rows, count):
        keys = count * tokens
        s = lax.dot_general(
            q, cat[:keys, :cols], (((1,), (1,)), ((), ())), preferred_element_type=jnp.float32
        )
        s = s + jnp.concatenate(rows, axis=1)
        top = jnp.max(s, axis=1, keepdims=True)
        p = jnp.exp(s - top).astype(jnp.bfloat16)
        return jnp.dot(p, cat[:keys], preferred_element_type=jnp.float32), top

    def store(j, view, acc, top):
        acc_buf[j, view] = acc
        top_buf[j, view] = jnp.broadcast_to(top, (tokens, cols))

    def merge(j, view, acc, top):
        old = top_buf[j, view][:, :1]
        new = jnp.maximum(old, top)
        return acc_buf[j, view] * jnp.exp(old - new) + acc * jnp.exp(top - new), new

    hard, easy = upper, 1 - upper

    def gather(cat, spots, listed, held):
        rows = []
        for slab, index, valid in spots:
            cat[len(rows) * tokens : (len(rows) + 1) * tokens, :cols] = slab
            rows.append(bias_row(index, valid))
        for code in listed:
            index, valid = code % VALID, code // VALID
            pick, view = index // views, index % views
            slab = held[0][pick % 2, view]
            for group in range(1, len(held)):
                slab = jnp.where(pick // 2 == group, held[group][pick % 2, view], slab)
            cat[len(rows) * tokens : (len(rows) + 1) * tokens, :cols] = slab
            rows.append(bias_row(index, valid))
        return rows

    def order_list(n):
        query_view, j = n // 2, n % 2
        codes, keys = [], []
        for off in range(1, views):
            view = (query_view + off) % views
            listed = listing[query_view, view, base + j]
            present = jnp.where(listed >= 0, 1, 0)
            far = present * (listed - base)
            after, before = jnp.where(far > 1, 1, 0), jnp.where(far < 0, 1, 0)
            group = (1 + upper) * after + (2 - upper) * before
            second = jnp.where((far == 1) | (far == 3) | (far == -1), 1, 0)
            codes.append((2 * group + second) * views + view + VALID * present)
            keys.append(group * views + off)
        ranks = []
        for a in keys:
            ranks.append(sum(jnp.where(b < a, 1, 0) for b in keys if b is not a))
        for place_ in range(LISTED):
            table[n, place_] = sum(jnp.where(r == place_, c, 0) for r, c in zip(ranks, codes))

    def relay_step(step, carry):
        view = visit(step)

        @pl.when(step >= 1)
        def _():
            kv_from(view, 0).wait_recv()

        kv_from(view, 1).wait_recv()
        halo(view).start()
        for j in range(2):
            order_list(2 * step + j)
        return carry

    lax.fori_loop(0, views, relay_step, 0)

    def own_step(step, carry):
        view = visit(step)
        halo(view).wait_recv()
        cross(view).start()

        @pl.when(step >= 1)
        def _():
            q_from(view, 0).wait_recv()

        q_from(view, 1).wait_recv()
        for n, j in enumerate((hard, easy)):
            spots = [(kv_own[0, view], view, 1), (kv_own[1, view], views + view, 1)]
            if n == 1:
                spots.append((kv_side[upper, view], (2 + upper) * views + view, 1))
            rows = gather(cats[n], spots, [table[2 * view + j, r] for r in range(FIRST)], (kv_own,))
            store(j, view, *attend(cats[n], query(j, view), rows, len(rows)))
        return carry

    lax.fori_loop(0, views, own_step, 0)

    def near_step(i, carry):
        for turn_ in range(AT_ONCE):
            view = visit(views - 1 - AT_ONCE * i - turn_)
            for n, (j, count) in enumerate(((hard, HARD), (easy, EASY))):
                cat = cats[2 * turn_ + n]
                rows = gather(cat, [], [table[2 * view + j, r] for r in range(FIRST, count)], (kv_own, kv_side))
                acc, top = attend(cat, query(j, view), rows, len(rows))
                store(j, view, *merge(j, view, acc, top))
        return carry

    lax.fori_loop(0, views // AT_ONCE, near_step, 0)

    for step in range(views):
        cross(visit(step)).wait_recv()

    def far_step(i, carry):
        for turn_ in range(AT_ONCE):
            view = visit(views - 1 - AT_ONCE * i - turn_)
            for n, (j, count) in enumerate(((hard, HARD), (easy, EASY))):
                cat = cats[2 * turn_ + n]
                spots = []
                if n == 0:
                    there = jnp.where(upper > 0, jnp.where(base + 2 < bands, 1, 0), jnp.where(base > 0, 1, 0))
                    spots.append((kv_far[1 - upper, view], (5 - upper) * views + view, there))
                listed = [table[2 * view + j, r] for r in range(count, LISTED)]
                rows = gather(cat, spots, listed, (kv_own, kv_side, kv_far))
                acc, top = attend(cat, query(j, view), rows, len(rows))
                total, _ = merge(j, view, acc, top)
                blend = total[:, :cols] / total[:, cols:]
                packed = jnp.where(low_part, turn(blend[:part_rows]), blend[part_rows:])
                o_send[j, view] = packed.astype(jnp.bfloat16)
        for turn_ in range(AT_ONCE):
            nth = AT_ONCE * i + turn_
            view = visit(views - 1 - nth)
            o_to(view, 1 - odd).start()

            @pl.when(nth < views - 1)
            def _():
                o_to(view, odd).start()

        return carry

    lax.fori_loop(0, views // AT_ONCE, far_step, 0)
    o_buf[2 * me + head] = o_send[odd, me]
    for view in others:
        o_from(view, 0).wait_recv()
    for view in [me, *others]:
        o_from(view, 1).wait_recv()

    for g in range(views):
        a, b = o_buf[2 * g].astype(jnp.float32), o_buf[2 * g + 1].astype(jnp.float32)
        both = jnp.concatenate([jnp.where(low_part, a, turn(b)), jnp.where(low_part, turn(a), b)], axis=0)
        out[:, g * cols : (g + 1) * cols] = both.astype(jnp.bfloat16)

    for view in others:
        for theirs in range(2):
            kv_to(view, theirs).wait_send()
            q_to(view, theirs).wait_send()
        for j in range(2):
            o_to(view, j).wait_send()
    kv_to(me, 1).wait_send()
    q_to(me, 1).wait_send()
    o_to(me, 1 - odd).wait_send()
    for view in [me, *others]:
        halo(view).wait_send()
        cross(view).wait_send()


def body(latents, w_qkv, w_out, epipolar_bands, object_token_mask):
    views = lax.axis_size("view")
    bands = lax.axis_size("band")
    tokens, width = latents.shape[1:]
    cols = width // views
    bf16, f32 = jnp.bfloat16, jnp.float32
    dma = pltpu.SemaphoreType.DMA
    vmem = pl.BlockSpec(memory_space=pltpu.VMEM)
    hbm = pl.BlockSpec(memory_space=pltpu.HBM)
    blended = pl.pallas_call(
        functools.partial(kernel, views, bands),
        out_shape=jax.ShapeDtypeStruct((tokens, width), bf16),
        in_specs=[pl.BlockSpec(memory_space=pltpu.SMEM), hbm, hbm, hbm],
        out_specs=vmem,
        scratch_shapes=[
            pltpu.SMEM((2 * views, LISTED), jnp.int32),
            pltpu.VMEM((tokens, width), bf16),
            pltpu.VMEM((views // 2, 3, width, 2 * cols), bf16),
            pltpu.VMEM((6 * views, tokens), jnp.int32),
            pltpu.VMEM((views, 2, tokens, cols), bf16),
            pltpu.VMEM((views, 2, tokens // 2, cols), bf16),
            *[pltpu.VMEM((2, views, tokens, cols), bf16) for _ in range(3)],
            pltpu.VMEM((2, views, tokens // 2, cols), bf16),
            *[pltpu.VMEM(((LISTED - 1) * tokens, 2 * cols), bf16) for _ in range(CATS)],
            pltpu.VMEM((2, views, tokens, 2 * cols), f32),
            pltpu.VMEM((2, views, tokens, cols), f32),
            pltpu.VMEM((2, views, tokens // 2, cols), bf16),
            pltpu.VMEM((2 * views, tokens // 2, cols), bf16),
            dma,
            dma((views // 2, 3)),
            dma((6,)),
            dma((views, 2)),
            dma((2, views)),
            dma((views, 2)),
            dma((2, views)),
            dma((views,)),
            dma((views,)),
            dma((views,)),
            dma((views,)),
            dma((2, views)),
            dma((2 * views,)),
        ],
        compiler_params=pltpu.CompilerParams(
            collective_id=0, has_side_effects=True, vmem_limit_bytes=60 * 2**20
        ),
    )(epipolar_bands.transpose(0, 2, 1), latents[0], w_qkv, object_token_mask)
    updated = latents[0].astype(f32) + jnp.dot(blended, w_out, preferred_element_type=f32)
    return updated[None]


def solution(mesh):
    placed = (P("view", "band", None), P(), P(), P(), P())
    return jax.shard_map(
        body, mesh=mesh, in_specs=placed, out_specs=P("view", "band", None), check_vma=False
    )
```
